32 devices in a mesh: sec: 4 (over x, core), elem: 8 (over z, y).
Axes of the slice: x: 2, y: 2, z: 4, core: 2. Of those that a mesh axis runs over, the one named last changes fastest.
Arguments:
- thermal_level_points: float32 [4, 8, 8, 8, 1024], P('sec', None, None, None, 'elem'), may hold values from -6 to 6
- flow_speed_vector: float32 [3, 4, 8, 8, 8, 1024], P(None, 'sec', None, None, None, 'elem'), may hold values from -3 to 3
- thermal_diffusivity_cell: float32 [4, 1024], P('sec', 'elem'), may hold values from 0.3 to 3
- metal_cell_indicator: int32 [4, 1024], P('sec', 'elem'), may hold values 0 or 1
- adjoining_patch: int32 [4, 1024], P('sec', 'elem'), may hold values from 0 to 3, as said below
Outputs:
- temperature_out: float32 [4, 8, 8, 8, 1024], P('sec', None, None, None, 'elem')
The draws below stay inside these ranges and needn't reach their ends.
Inputs may be any that keep to these rules, and one draw needn't show every extreme that they name: adjoining_patch[adjoining_patch[s, e], e] = s and adjoining_patch[s, e] != s: at every chain position the sections are paired; within each aligned block of 128 chain positions a pair of sections shares at most 43 positions, and some pair shares exactly 43.
All inputs are finite; a program needn't handle non-finite values. No bound on the sum of `metal_cell_indicator` on one device may be relied on, other than what follows from the above.
Results may differ from the reference program's by a relative error of at most 0.0001.
Values sent between devices are 32-bit elements; how exact they have to be, the bound alone decides.
No kernel may reach another device: no remote copies, remote signals or barrier semaphores. Data moves between devices by JAX's collectives and lax.ppermute only.
A program may use at most 64 MiB of HBM per device.

```python
import math
import jax
import jax.numpy as jnp
import numpy as np
from jax import lax

LINE_POINT_TOTAL = 8
FINE = 11
ELEM_DEV = 128
SWEEPS = 4
STEPS = 2
PATCH_CELLS = 1024
N_SEC = 4


def draw_adjoining_patch(key, part):
    block_count = PATCH_CELLS // ELEM_DEV
    block_keys = jax.random.split(jax.random.fold_in(key, 17), block_count)
    orders = jax.vmap(lambda single_key: jax.random.permutation(single_key, ELEM_DEV))(block_keys)
    mate_code = (orders.astype(jnp.int32) % (N_SEC - 1) + 1).reshape((PATCH_CELLS,))
    sections = jnp.arange(N_SEC, dtype=jnp.int32)
    return jnp.bitwise_xor(sections[:, None], mate_code[None, :]).astype(jnp.int32)


def set_ends(array, stream_key, least, largest):
    place = [jax.random.randint(jax.random.fold_in(stream_key, axis), (), 0, length) for axis, length in enumerate(array.shape)]
    longest = array.shape.index(max(array.shape))
    next_to = place[:longest] + [(place[longest] + 1) % array.shape[longest]] + place[longest + 1:]
    return array.at[tuple(place)].set(least).at[tuple(next_to)].set(largest)


def level_of(rng, shape, cuts, low, top_value):
    def one(position, parts):
        steps = jax.random.uniform(jax.random.fold_in(jax.random.fold_in(rng, 6), position), (parts,), jnp.float32, low / len(cuts), top_value / len(cuts))
        return jnp.repeat(jnp.exp(steps), shape[position] // parts).reshape((-1,) + (1,) * (len(shape) - position - 1))

    factor_of = one(*cuts[0])
    for cut in cuts[1:]:
        factor_of = factor_of * one(*cut)
    return factor_of


def bell_draw(stream_key, dims, spread, most, shards=(), held_as=jnp.bfloat16):
    values = spread * jax.random.normal(stream_key, dims, jnp.float32)
    if shards:
        values = values * level_of(stream_key, dims, shards, -0.22, 0.18)
    return jnp.clip(values, -most, most).astype(held_as)


def setup_inputs(seed: int = 0) -> dict:
    seeds = jax.random.split(jax.random.key(seed), 6)
    return {
        "thermal_level_points": bell_draw(seeds[0], (N_SEC, LINE_POINT_TOTAL, LINE_POINT_TOTAL, LINE_POINT_TOTAL, PATCH_CELLS), 1.0, 6.0, ((0, 4), (4, 8)), jnp.float32),
        "flow_speed_vector": bell_draw(seeds[1], (3, N_SEC, LINE_POINT_TOTAL, LINE_POINT_TOTAL, LINE_POINT_TOTAL, PATCH_CELLS), 0.5, 3.0, ((1, 4), (5, 8)), jnp.float32),
        "thermal_diffusivity_cell": jnp.clip(jnp.exp(math.log(3.0) - 2.3025851 * jax.random.uniform(seeds[2], (N_SEC, PATCH_CELLS), jnp.float32) ** level_of(seeds[2], (N_SEC, PATCH_CELLS), ((0, 4), (1, 8)), -0.2, 0.2)), 0.3, 3.0),
        "metal_cell_indicator": set_ends((jax.random.randint(seeds[3], (N_SEC, PATCH_CELLS), 0, 5) < 1).astype(jnp.int32), jax.random.fold_in(seeds[3], 1), 0, 1),
        "adjoining_patch": draw_adjoining_patch(jax.random.fold_in(seeds[5], 71), 0),
    }


highest = lax.Precision.HIGHEST
time_step = 0.05
relaxation = 0.4
penalty = 30.0


def legendre_pair(order, points):
    previous = points * 0.0 + 1.0
    current = points * 1.0
    for level in range(2, order + 1):
        previous, current = current, ((2 * level - 1) * points * current - (level - 1) * previous) / level
    return current, previous


def make_tables():
    degree = LINE_POINT_TOTAL - 1
    gll_nodes = -np.cos(np.pi * np.arange(LINE_POINT_TOTAL) / degree)
    for repeat in range(100):
        current, previous = legendre_pair(degree, gll_nodes)
        gll_nodes = gll_nodes - (gll_nodes * current - previous) / (LINE_POINT_TOTAL * current)
    values, lower_values = legendre_pair(degree, gll_nodes)
    weights = 2.0 / (degree * (degree + 1) * values ** 2)
    spatial_derivative = np.zeros((LINE_POINT_TOTAL, LINE_POINT_TOTAL))
    for row_index in range(LINE_POINT_TOTAL):
        for column_index in range(LINE_POINT_TOTAL):
            if row_index != column_index:
                spatial_derivative[row_index, column_index] = values[row_index] / (values[column_index] * (gll_nodes[row_index] - gll_nodes[column_index]))
    spatial_derivative[0, 0] = -degree * (degree + 1) / 4.0
    spatial_derivative[-1, -1] = degree * (degree + 1) / 4.0
    fine_nodes = -np.cos(np.pi * (np.arange(FINE) + 0.75) / (FINE + 0.5))
    for repeat in range(100):
        current, previous = legendre_pair(FINE, fine_nodes)
        slope = FINE * (fine_nodes * current - previous) / (fine_nodes * fine_nodes - 1.0)
        fine_nodes = fine_nodes - current / slope
    current, previous = legendre_pair(FINE, fine_nodes)
    slope = FINE * (fine_nodes * current - previous) / (fine_nodes * fine_nodes - 1.0)
    fine_weights = 2.0 / ((1.0 - fine_nodes * fine_nodes) * slope * slope)
    interpolation = np.ones((FINE, LINE_POINT_TOTAL))
    for column_index in range(LINE_POINT_TOTAL):
        for other_index in range(LINE_POINT_TOTAL):
            if other_index != column_index:
                interpolation[:, column_index] *= (fine_nodes - gll_nodes[other_index]) / (gll_nodes[column_index] - gll_nodes[other_index])
    stiffness_1d = spatial_derivative.T @ (weights[:, None] * spatial_derivative)
    return (jnp.asarray(spatial_derivative, jnp.float32), jnp.asarray(interpolation, jnp.float32),
            jnp.asarray(stiffness_1d, jnp.float32), jnp.asarray(weights, jnp.float32),
            jnp.asarray(fine_weights, jnp.float32))


def act_along_coordinate(matrix, grid_values, coordinate_axis_label):
    if coordinate_axis_label == 0:
        return jnp.einsum("qa,sabce->sqbce", matrix, grid_values, precision=highest)
    if coordinate_axis_label == 1:
        return jnp.einsum("qb,sabce->saqce", matrix, grid_values, precision=highest)
    return jnp.einsum("qc,sabce->sabqe", matrix, grid_values, precision=highest)


def lift_fine(matrix, grid_values):
    result = grid_values
    for coordinate_axis_label in range(3):
        result = act_along_coordinate(matrix, result, coordinate_axis_label)
    return result


def point_weights(weights):
    return (weights[None, :, None, None, None], weights[None, None, :, None, None], weights[None, None, None, :, None])


def mass_grid(weights):
    weight_a, weight_b, weight_c = point_weights(weights)
    return weight_a * weight_b * weight_c


def transport_flux(thermal_level_points, flow_speed_vector, liquid_cell_indicator, spectral_matrix_bundle):
    spatial_derivative, interpolation, stiffness_1d, weights, fine_weights = spectral_matrix_bundle
    fluid_grid = liquid_cell_indicator[:, None, None, None, :]
    product_sum = None
    for coordinate_axis_label in range(3):
        slope_vector_values = act_along_coordinate(spatial_derivative, thermal_level_points, coordinate_axis_label)
        term = lift_fine(interpolation, flow_speed_vector[coordinate_axis_label] * fluid_grid) * lift_fine(interpolation, slope_vector_values)
        product_sum = term if coordinate_axis_label == 0 else product_sum + term
    cube = fine_weights[:, None, None] * fine_weights[None, :, None] * fine_weights[None, None, :]
    return lift_fine(interpolation.T, product_sum * cube[None, :, :, :, None])


def stiffness_apply(grid_values, spectral_matrix_bundle):
    stiffness_1d = spectral_matrix_bundle[2]
    weight_a, weight_b, weight_c = point_weights(spectral_matrix_bundle[3])
    return (act_along_coordinate(stiffness_1d, grid_values, 0) * (weight_b * weight_c)
            + act_along_coordinate(stiffness_1d, grid_values, 1) * (weight_a * weight_c)
            + act_along_coordinate(stiffness_1d, grid_values, 2) * (weight_a * weight_b))


def face_terms(grid_values, near_minus, near_plus, far_wall, coefficients, spectral_matrix_bundle):
    coef_left, coef_right, coef_wall = coefficients
    weights = spectral_matrix_bundle[3]
    face_weight = (weights[:, None] * weights[None, :])[None, :, :, None]
    result = jnp.zeros_like(grid_values)
    result = result.at[:, 0].add(coef_left[:, None, None, :] * face_weight * (grid_values[:, 0] - near_plus))
    result = result.at[:, -1].add(coef_right[:, None, None, :] * face_weight * (grid_values[:, -1] - near_minus))
    result = result.at[:, :, :, 0].add(coef_wall[:, None, None, :] * face_weight * (grid_values[:, :, :, 0] - far_wall))
    return result


def diagonal_h(thermal_diffusivity_cell, coefficients, spectral_matrix_bundle):
    coef_left, coef_right, coef_wall = coefficients
    stiffness_1d, weights = spectral_matrix_bundle[2], spectral_matrix_bundle[3]
    weight_a, weight_b, weight_c = point_weights(weights)
    stiff_diag = jnp.diagonal(stiffness_1d)
    k_diag = (stiff_diag[None, :, None, None, None] * weight_b * weight_c
              + weight_a * stiff_diag[None, None, :, None, None] * weight_c
              + weight_a * weight_b * stiff_diag[None, None, None, :, None])
    result = mass_grid(weights) / time_step + thermal_diffusivity_cell[:, None, None, None, :] * k_diag
    face_weight = (weights[:, None] * weights[None, :])[None, :, :, None]
    result = result.at[:, 0].add(coef_left[:, None, None, :] * face_weight)
    result = result.at[:, -1].add(coef_right[:, None, None, :] * face_weight)
    result = result.at[:, :, :, 0].add(coef_wall[:, None, None, :] * face_weight)
    return result


def sweep_update(iterate, right_side, diagonal, faces_part, thermal_diffusivity_cell, spectral_matrix_bundle):
    applied = (mass_grid(spectral_matrix_bundle[3]) / time_step * iterate
               + thermal_diffusivity_cell[:, None, None, None, :] * stiffness_apply(iterate, spectral_matrix_bundle) + faces_part)
    return iterate + relaxation * (right_side - applied) / diagonal


def reference(thermal_level_points, flow_speed_vector, thermal_diffusivity_cell, metal_cell_indicator, adjoining_patch):
    spectral_matrix_bundle = make_tables()
    padded = jnp.pad(thermal_diffusivity_cell, ((0, 0), (1, 1)))
    chain_index = jnp.arange(thermal_diffusivity_cell.shape[1], dtype=jnp.int32)
    coef_right = jnp.where(chain_index < PATCH_CELLS - 1, penalty * (thermal_diffusivity_cell + padded[:, 2:]) * 0.5, 0.0)
    coef_left = jnp.where(chain_index > 0, penalty * (thermal_diffusivity_cell + padded[:, :-2]) * 0.5, 0.0)
    partner_k = jnp.take_along_axis(thermal_diffusivity_cell, adjoining_patch, axis=0)
    partner_solid = jnp.take_along_axis(metal_cell_indicator, adjoining_patch, axis=0)
    coef_wall = jnp.where(metal_cell_indicator != partner_solid, penalty * (thermal_diffusivity_cell + partner_k) * 0.5, 0.0)
    coefficients = (coef_left, coef_right, coef_wall)
    liquid_cell_indicator = 1.0 - metal_cell_indicator.astype(jnp.float32)
    diagonal = diagonal_h(thermal_diffusivity_cell, coefficients, spectral_matrix_bundle)
    moved_velocity = jnp.moveaxis(flow_speed_vector, 1, 0)

    def per_section(section_data):
        temp_section, velocity_section, fluid_section = section_data
        return transport_flux(temp_section[None], velocity_section[:, None], fluid_section[None], spectral_matrix_bundle)[0]

    iteration_snapshot = thermal_level_points
    for step_index in range(STEPS):
        convected = lax.map(per_section, (iteration_snapshot, moved_velocity, liquid_cell_indicator))
        right_side = mass_grid(spectral_matrix_bundle[3]) / time_step * iteration_snapshot - convected
        iterate = iteration_snapshot
        for sweep_index in range(SWEEPS):
            near_minus = jnp.pad(iterate[:, 0], ((0, 0), (0, 0), (0, 0), (0, 1)))[..., 1:]
            near_plus = jnp.pad(iterate[:, -1], ((0, 0), (0, 0), (0, 0), (1, 0)))[..., :-1]
            wall_face = iterate[:, :, :, 0]
            index_grid = jnp.broadcast_to(adjoining_patch[:, None, None, :], wall_face.shape)
            far_wall = jnp.take_along_axis(wall_face, index_grid, axis=0)
            faces_part = face_terms(iterate, near_minus, near_plus, far_wall, coefficients, spectral_matrix_bundle)
            iterate = sweep_update(iterate, right_side, diagonal, faces_part, thermal_diffusivity_cell, spectral_matrix_bundle)
        iteration_snapshot = iterate
    return iteration_snapshot
```

```python
import functools

import jax
import jax.numpy as jnp
import ml_dtypes
import numpy as np
from jax import lax
from jax.experimental import pallas as pl
from jax.experimental.pallas import tpu as pltpu
from jax.sharding import PartitionSpec as P

LINE_POINT_TOTAL = 8
FINE = 11
SWEEPS = 4
STEPS = 2
GHOST = STEPS * SWEEPS

time_step = 0.05
relaxation = 0.4
penalty = 30.0

POINTS = LINE_POINT_TOTAL**3
FIELDS = 4
PARAM_ROWS = 8
LANES = 128
HALF = LINE_POINT_TOTAL // 2
MIRROR = FINE // 2
CLASSES = ((0, 0), (0, 1), (1, 0), (1, 1))
CLASS_ROWS = HALF * HALF * LINE_POINT_TOTAL


def round_up(value, unit):
    return -(-value // unit) * unit


PAIR_ROWS = round_up(MIRROR * FINE, 8)
MID_ROWS = round_up(FINE, 8)
SLAB_ROWS = 2 * PAIR_ROWS + MID_ROWS
FINE_C_ROWS = (PAIR_ROWS + MID_ROWS, PAIR_ROWS)
FINE_A_COUNT = (MIRROR + 1, MIRROR)


def class_fine_rows(cls):
    return round_up(FINE_A_COUNT[cls[0]] * FINE_C_ROWS[cls[1]], 16)


def legendre_pair(order, points):
    previous = points * 0.0 + 1.0
    current = points * 1.0
    for level in range(2, order + 1):
        previous, current = (
            current,
            ((2 * level - 1) * points * current - (level - 1) * previous) / level,
        )
    return (current, previous)


def make_tables():
    degree = LINE_POINT_TOTAL - 1
    gll_nodes = -np.cos(np.pi * np.arange(LINE_POINT_TOTAL) / degree)
    for repeat in range(100):
        current, previous = legendre_pair(degree, gll_nodes)
        gll_nodes = gll_nodes - (gll_nodes * current - previous) / (LINE_POINT_TOTAL * current)
    values, lower_values = legendre_pair(degree, gll_nodes)
    weights = 2.0 / (degree * (degree + 1) * values**2)
    spatial_derivative = np.zeros((LINE_POINT_TOTAL, LINE_POINT_TOTAL))
    for row_index in range(LINE_POINT_TOTAL):
        for column_index in range(LINE_POINT_TOTAL):
            if row_index != column_index:
                spatial_derivative[row_index, column_index] = values[row_index] / (
                    values[column_index] * (gll_nodes[row_index] - gll_nodes[column_index])
                )
    spatial_derivative[0, 0] = -degree * (degree + 1) / 4.0
    spatial_derivative[-1, -1] = degree * (degree + 1) / 4.0
    fine_nodes = -np.cos(np.pi * (np.arange(FINE) + 0.75) / (FINE + 0.5))
    for repeat in range(100):
        current, previous = legendre_pair(FINE, fine_nodes)
        slope = FINE * (fine_nodes * current - previous) / (fine_nodes * fine_nodes - 1.0)
        fine_nodes = fine_nodes - current / slope
    current, previous = legendre_pair(FINE, fine_nodes)
    slope = FINE * (fine_nodes * current - previous) / (fine_nodes * fine_nodes - 1.0)
    fine_weights = 2.0 / ((1.0 - fine_nodes * fine_nodes) * slope * slope)
    interpolation = np.ones((FINE, LINE_POINT_TOTAL))
    for column_index in range(LINE_POINT_TOTAL):
        for other_index in range(LINE_POINT_TOTAL):
            if other_index != column_index:
                interpolation[:, column_index] *= (fine_nodes - gll_nodes[other_index]) / (
                    gll_nodes[column_index] - gll_nodes[other_index]
                )
    stiffness_1d = spatial_derivative.T @ (weights[:, None] * spatial_derivative)
    return spatial_derivative, interpolation, stiffness_1d, weights, fine_weights


def parity_parts(matrix, out_rows, sign):
    near = matrix[:out_rows, :HALF]
    far = matrix[:out_rows, ::-1][:, :HALF]
    return (near + sign * far) * 0.5


def fine_matrix(cls, line_a, line_b, line_c):
    count_c = FINE_A_COUNT[cls[1]]
    full = np.einsum("xa,yc,zb->xyzacb", line_a, line_c, line_b)
    full = full.reshape(FINE_A_COUNT[cls[0]], count_c, FINE, CLASS_ROWS)
    slabs = np.zeros((FINE_A_COUNT[cls[0]], FINE_C_ROWS[cls[1]], CLASS_ROWS))
    slabs[:, : MIRROR * FINE] = full[:, :MIRROR].reshape(-1, MIRROR * FINE, CLASS_ROWS)
    if cls[1] == 0:
        slabs[:, PAIR_ROWS : PAIR_ROWS + FINE] = full[:, MIRROR]
    result = np.zeros((class_fine_rows(cls), CLASS_ROWS))
    result[: slabs.shape[0] * slabs.shape[1]] = slabs.reshape(-1, CLASS_ROWS)
    return result


def split_stack(matrix):
    high = matrix.astype(ml_dtypes.bfloat16)
    low = (matrix - high.astype(np.float64)).astype(ml_dtypes.bfloat16)
    return np.concatenate(
        [np.concatenate([high, high], 1), np.concatenate([low, low], 1)], 0
    )


def make_matrices():
    derivative, interpolation, stiffness, weights, fine_weights = make_tables()
    slope = interpolation @ derivative
    even = parity_parts(interpolation, MIRROR + 1, 1.0)
    odd = parity_parts(interpolation, MIRROR, -1.0)
    slope_even = parity_parts(slope, MIRROR + 1, -1.0)
    slope_odd = parity_parts(slope, MIRROR, 1.0)
    plain, steep = (even, odd), (slope_even, slope_odd)
    lifts = []
    for direction in (None, 0, 1, 2):
        for cls in CLASSES:
            line_a = (steep if direction == 0 else plain)[cls[0]]
            line_c = (steep if direction == 2 else plain)[cls[1]]
            line_b = slope if direction == 1 else interpolation
            lifts.append(split_stack(fine_matrix(cls, line_a, line_b, line_c)))
    backs = []
    for cls in CLASSES:
        lines = []
        for parity in cls:
            rows = FINE_A_COUNT[parity]
            lines.append(plain[parity] * fine_weights[:rows, None])
        backs.append(
            split_stack(
                fine_matrix(cls, lines[0], interpolation * fine_weights[:, None], lines[1]).T
            )
        )
    stiff = []
    for cls in CLASSES:
        parts = [
            parity_parts(stiffness, HALF, 1.0 - 2.0 * parity)[:HALF] for parity in cls
        ]
        mass = np.diag(weights[:HALF]) * 0.5
        total = (
            np.einsum("ij,kl,mn->ikmjln", parts[0], mass, np.diag(weights))
            + np.einsum("ij,kl,mn->ikmjln", mass, parts[1], np.diag(weights))
            + np.einsum("ij,kl,mn->ikmjln", mass, mass, stiffness)
        )
        stiff.append(split_stack(total.reshape(CLASS_ROWS, CLASS_ROWS)))
    return lifts, backs, stiff


def pair_of(here, shift, count):
    if count & (count - 1) == 0:
        return here ^ shift
    return (here + shift) % count


class Layout:
    def __init__(self, elements, sections):
        self.elements = elements
        self.sections = sections
        self.main = elements // sections
        self.slot = self.main + 2 * GHOST
        while (self.slot * sections) % LANES:
            self.slot += 1
        self.columns = self.slot * sections
        self.main_rows = POINTS // sections
        self.ghost_groups = elements // (2 * GHOST)
        self.ghost_rows = POINTS // self.ghost_groups
        self.end_groups = elements // GHOST
        self.end_rows = POINTS // self.end_groups
        apart = self.main + GHOST
        self.joint = apart % (2 * GHOST) == GHOST
        self.right_offset = apart if self.joint else GHOST

    def window_pieces(self, source, target, width):
        pieces = []
        done = 0
        while done < width:
            at, to = source + done, target + done
            step = min(width - done, LANES - at % LANES, LANES - to % LANES)
            first = to % LANES
            pieces.append((at // LANES, to // LANES, (to - at) % LANES, first, first + step))
            done += step
        return pieces


def lane_iota(rows):
    return lax.broadcasted_iota(jnp.int32, (rows, LANES), 1)


def in_range(lane, first, last):
    return (lane >= first) & (lane < last)


def turned(value, shift):
    if isinstance(shift, int) and shift % value.shape[-1] == 0:
        return value
    return pltpu.roll(value, shift, axis=1)


def reorder(temperature, velocity, ordered):
    for field in range(FIELDS):
        source = temperature if field == 0 else velocity.at[field - 1]
        for a in range(LINE_POINT_TOTAL):
            for c in range(LINE_POINT_TOTAL):
                base = a * 64 + c
                ordered[field, pl.ds((a * 8 + c) * 8, 8), :] = source[pl.ds(base, 8, stride=8), :]


def pack_main_kernel(layout, scalars, temperature, velocity, params, *rest):
    outs = rest[: layout.sections]
    low_end, high_end, ordered = rest[layout.sections :]
    reorder(temperature, velocity, ordered)
    here = scalars[0]
    elements, main, rows = layout.elements, layout.main, layout.main_rows
    lane = lane_iota(rows)
    for shift in range(layout.sections):
        there = pair_of(here, shift, layout.sections)
        for field in range(FIELDS):
            value = None
            for group in range(layout.sections):
                amount = lax.rem((group - there) * main + elements, elements)
                part = pltpu.roll(ordered[field, pl.ds(group * rows, rows), :], amount, axis=1)
                value = (
                    part
                    if value is None
                    else jnp.where(in_range(lane, group * main, (group + 1) * main), part, value)
                )
            outs[shift][pl.ds(field * rows, rows), :] = value
        outs[shift][pl.ds(FIELDS * rows, PARAM_ROWS), :] = pltpu.roll(
            params[...], lax.rem(elements - there * main, elements), axis=1
        )
    rows = layout.end_rows
    lane = lane_iota(rows)
    for out, first in ((low_end, 0), (high_end, elements - GHOST)):
        for field in range(FIELDS):
            value = None
            for group in range(layout.end_groups):
                part = turned(
                    ordered[field, pl.ds(group * rows, rows), :],
                    (group * GHOST - first) % elements,
                )
                value = (
                    part
                    if value is None
                    else jnp.where(in_range(lane, group * GHOST, (group + 1) * GHOST), part, value)
                )
            out[pl.ds(field * rows, rows), :] = value
        out[pl.ds(FIELDS * rows, PARAM_ROWS), :] = turned(params[...], (-first) % elements)


def pack_ghost_kernel(
    layout, scalars, ordered, params, from_low, from_high, *rest
):
    outs, edge = rest[: layout.sections], rest[layout.sections]
    here = scalars[0]
    elements, main, sections = layout.elements, layout.main, layout.sections
    rows = layout.end_rows
    lane = lane_iota(rows)
    for field in range(FIELDS):
        for group in range(layout.end_groups):
            low = turned(from_low[pl.ds(field * rows, rows), :], (-GHOST - group * GHOST) % elements)
            high = turned(from_high[pl.ds(field * rows, rows), :], (-group * GHOST) % elements)
            edge[field, pl.ds(group * rows, rows), :] = jnp.where(lane < elements // 2, high, low)
    low = turned(from_low[pl.ds(FIELDS * rows, PARAM_ROWS), :], elements - GHOST)
    high = from_high[pl.ds(FIELDS * rows, PARAM_ROWS), :]
    edge_params = jnp.where(lane_iota(PARAM_ROWS) < elements // 2, high, low)
    rows = layout.ghost_rows
    lane = lane_iota(rows)

    def gather(inner, outer, first, last, group, there, mask_lane, value):
        left = jnp.where(first, outer, inner)
        right = jnp.where(last, outer, inner)
        shift_left = lax.rem(2 * GHOST * group + GHOST - main * there + elements, elements)
        at_left = 2 * GHOST * group
        at_right = (2 * GHOST * group + layout.right_offset) % elements
        left_mask = in_range(mask_lane, at_left, at_left + GHOST)
        right_mask = in_range(mask_lane, at_right, at_right + GHOST)
        if layout.joint:
            source_lane = lax.rem(mask_lane - main * there + elements + GHOST, elements)
            both = jnp.where(source_lane < GHOST, left, right)
            part = pltpu.roll(both, shift_left, axis=1)
            return jnp.where(left_mask | right_mask, part, value)
        shift_right = lax.rem(
            2 * GHOST * group + layout.right_offset - main * (there + 1) + 2 * elements, elements
        )
        value = jnp.where(left_mask, pltpu.roll(left, shift_left, axis=1), value)
        return jnp.where(right_mask, pltpu.roll(right, shift_right, axis=1), value)

    for shift in range(sections):
        there = pair_of(here, shift, sections)
        first, last = there == 0, there == sections - 1
        for field in range(FIELDS):
            value = jnp.zeros((rows, LANES), jnp.float32)
            for group in range(layout.ghost_groups):
                span = pl.ds(group * rows, rows)
                value = gather(
                    ordered[field, span, :], edge[field, span, :], first, last, group, there, lane, value
                )
            outs[shift][pl.ds(field * rows, rows), :] = value
        outs[shift][pl.ds(FIELDS * rows, PARAM_ROWS), :] = gather(
            params[...],
            edge_params,
            first,
            last,
            0,
            there,
            lane_iota(PARAM_ROWS),
            jnp.zeros((PARAM_ROWS, LANES), jnp.float32),
        )


def unpack_columns(layout, mains, ghosts, fields, param_value):
    sections, main, slot = layout.sections, layout.main, layout.slot
    tiles = layout.columns // LANES

    def moves(section, group, ghost):
        if not ghost:
            return layout.window_pieces(group * main, section * slot + GHOST, main)
        at_left = 2 * GHOST * group
        at_right = (at_left + layout.right_offset) % layout.elements
        return layout.window_pieces(at_left, section * slot, GHOST) + layout.window_pieces(
            at_right, section * slot + GHOST + main, GHOST
        )

    def fill(sources, rows, first_row, group, ghost, values):
        lane = lane_iota(rows)
        for section in range(sections):
            block = sources[section][pl.ds(first_row, rows), :]
            cache = {}
            for _, tile, shift, first, last in moves(section, group, ghost):
                if shift not in cache:
                    cache[shift] = turned(block, shift)
                mask = in_range(lane, first, last)
                values[tile] = jnp.where(mask, cache[shift], values[tile])
        return values

    def zeros(rows):
        return [jnp.zeros((rows, LANES), jnp.float32) for _ in range(tiles)]

    rows = min(layout.main_rows, layout.ghost_rows)
    for field in range(FIELDS):
        for start in range(0, POINTS, rows):
            group, offset = divmod(start, layout.main_rows)
            values = fill(
                mains, rows, field * layout.main_rows + offset, group, False, zeros(rows)
            )
            group, offset = divmod(start, layout.ghost_rows)
            values = fill(
                ghosts, rows, field * layout.ghost_rows + offset, group, True, values
            )
            for tile in range(tiles):
                fields[field, pl.ds(start, rows), pl.ds(tile * LANES, LANES)] = values[tile]
    values = fill(mains, PARAM_ROWS, FIELDS * layout.main_rows, 0, False, zeros(PARAM_ROWS))
    values = fill(ghosts, PARAM_ROWS, FIELDS * layout.ghost_rows, 0, True, values)
    for tile in range(tiles):
        param_value[:, pl.ds(tile * LANES, LANES)] = values[tile]


def store_split(target, row, half, value):
    high = value.astype(jnp.bfloat16)
    target[pl.ds(row, value.shape[0]), :] = high
    target[pl.ds(half + row, value.shape[0]), :] = (value - high.astype(jnp.float32)).astype(
        jnp.bfloat16
    )


def to_classes(source, pieces):
    for a in range(HALF):
        near = source[pl.ds(a * 64, 64), :]
        far = source[pl.ds((LINE_POINT_TOTAL - 1 - a) * 64, 64), :]
        for parity_a, slab in enumerate((near + far, near - far)):
            lower = slab[: HALF * 8]
            upper = jnp.concatenate(
                [slab[(LINE_POINT_TOTAL - 1 - c) * 8 :][:8] for c in range(HALF)], 0
            )
            for parity_c, part in enumerate((lower + upper, lower - upper)):
                store_split(pieces[2 * parity_a + parity_c], a * HALF * 8, CLASS_ROWS, part)


def multiply(matrix, pieces):
    product = jnp.dot(matrix[...], pieces[...], preferred_element_type=jnp.float32)
    half = product.shape[0] // 2
    return product[:half] + product[half:]


def from_classes(results, a):
    span = pl.ds(a * HALF * 8, HALF * 8)
    ee, eo, oe, oo = [results[index, span, :] for index in range(4)]

    def along_c(even, odd):
        lower, upper = even + odd, even - odd
        return jnp.concatenate(
            [lower] + [upper[c * 8 : c * 8 + 8] for c in reversed(range(HALF))], 0
        )

    return along_c(ee + oe, eo + oo), along_c(ee - oe, eo - oo)


def fine_slabs(fine, q):
    halves = []
    for parity_a in range(2):
        if q >= FINE_A_COUNT[parity_a]:
            break
        even = fine[2 * parity_a][pl.ds(q * FINE_C_ROWS[0], FINE_C_ROWS[0]), :]
        odd = fine[2 * parity_a + 1][pl.ds(q * FINE_C_ROWS[1], FINE_C_ROWS[1]), :]
        halves.append((even[:PAIR_ROWS] + odd, even[:PAIR_ROWS] - odd, even[PAIR_ROWS:]))
    if len(halves) == 1:
        return [halves[0]]
    return [
        tuple(x + y for x, y in zip(*halves)),
        tuple(x - y for x, y in zip(*halves)),
    ]


def main_kernel(layout, tables, *refs):
    weights = tables[3]
    sections, columns = layout.sections, layout.columns
    refs = list(refs)

    def take(count):
        taken, refs[:] = refs[:count], refs[count:]
        return taken

    mains, ghosts = take(sections), take(sections)
    lifts, backs, stiff = take(16), take(4), take(4)
    outs = take(sections)
    fields, param_value = take(2)
    fine = [take(4) for _ in range(3)]
    (lifted, point_pieces, results, keep, gain_rhs, gain_k, gain) = take(7)
    (gain_low, gain_high, gain_wall) = take(3)
    fine_pieces = take(4)
    pieces = [point_pieces.at[index] for index in range(4)]

    unpack_columns(layout, mains, ghosts, fields, param_value)

    params = param_value[...]
    k, metal, partner, has_low, has_high = [params[row : row + 1] for row in range(5)]

    def shifted(value, amount):
        return pltpu.roll(value, amount % columns, axis=1)

    lane = lax.broadcasted_iota(jnp.int32, (1, columns), 1)
    own_slot = lane // layout.slot
    partner_slot = pair_of(own_slot, partner.astype(jnp.int32), sections)
    distance = lax.rem(partner_slot - own_slot + sections, sections)
    coef_low = has_low * (0.5 * penalty) * (k + shifted(k, 1))
    coef_high = has_high * (0.5 * penalty) * (k + shifted(k, -1))
    partner_k, partner_metal = jnp.zeros_like(k), jnp.zeros_like(k)
    for step in range(1, sections):
        chosen = distance == step
        partner_k = jnp.where(chosen, shifted(k, -step * layout.slot), partner_k)
        partner_metal = jnp.where(chosen, shifted(metal, -step * layout.slot), partner_metal)
    coef_wall = jnp.where(metal != partner_metal, (0.5 * penalty) * (k + partner_k), 0.0)
    fluid = 1.0 - metal

    row = lax.broadcasted_iota(jnp.int32, (8, columns), 0)
    weight_b = jnp.zeros((8, columns), jnp.float32)
    stiff_b = jnp.zeros((8, columns), jnp.float32)
    stiff_line = np.diagonal(tables[2])
    for b in range(8):
        weight_b = jnp.where(row == b, float(weights[b]), weight_b)
        stiff_b = jnp.where(row == b, float(stiff_line[b]), stiff_b)
    last = LINE_POINT_TOTAL - 1
    for a in range(LINE_POINT_TOTAL):
        for c in range(LINE_POINT_TOTAL):
            wa, wc = float(weights[a]), float(weights[c])
            mass = weight_b * (wa * wc / time_step)
            diag = mass + k * (
                weight_b * (float(stiff_line[a]) * wc + wa * float(stiff_line[c]))
                + stiff_b * (wa * wc)
            )
            face = None
            if a == 0:
                face_low = coef_low * (weight_b * wc)
                face = face_low
            if a == last:
                face_high = coef_high * (weight_b * wc)
                face = face_high
            if c == 0:
                face_wall = coef_wall * (weight_b * wa)
                face = face_wall if face is None else face + face_wall
            if face is not None:
                diag = diag + face
            factor = relaxation / diag
            span = pl.ds((a * 8 + c) * 8, 8)
            gain[span, :] = factor
            gain_k[span, :] = factor * k
            keep[span, :] = 1.0 - factor * (mass if face is None else mass + face)
            if a == 0:
                gain_low[pl.ds(c * 8, 8), :] = factor * face_low
            if a == last:
                gain_high[pl.ds(c * 8, 8), :] = factor * face_high
            if c == 0:
                gain_wall[pl.ds(a * 8, 8), :] = factor * face_wall

    for direction in range(3):
        to_classes(fields.at[direction + 1], pieces)
        for index in range(4):
            fine[0][index][...] = multiply(lifts[index], pieces[index])
        for q in range(MIRROR + 1):
            for point, slab in zip((q, FINE - 1 - q), fine_slabs(fine[0], q)):
                base = 0
                for part in slab:
                    lifted[direction, point, pl.ds(base, part.shape[0]), :] = part
                    base += part.shape[0]

    iterate = fields.at[0]
    for step_index in range(STEPS):
        to_classes(iterate, pieces)
        for direction in range(3):
            for index, cls in enumerate(CLASSES):
                source = index ^ (2 if direction == 0 else 1 if direction == 2 else 0)
                fine[direction][index][...] = multiply(
                    lifts[4 * (direction + 1) + index], pieces[source]
                )
        pending = [[], [], [], []]
        done = [0, 0, 0, 0]
        for q in range(MIRROR + 1):
            products = None
            for direction in range(3):
                slabs = fine_slabs(fine[direction], q)
                terms = []
                for point, slab in zip((q, FINE - 1 - q), slabs):
                    base = 0
                    parts = []
                    for part in slab:
                        parts.append(
                            part * lifted[direction, point, pl.ds(base, part.shape[0]), :]
                        )
                        base += part.shape[0]
                    terms.append(parts)
                products = (
                    terms
                    if products is None
                    else [[x + y for x, y in zip(s, t)] for s, t in zip(products, terms)]
                )
            if len(products) == 2:
                halves = [
                    [x + y for x, y in zip(*products)],
                    [x - y for x, y in zip(*products)],
                ]
            else:
                halves = products
            for parity_a, (plus, minus, middle) in enumerate(halves):
                pending[2 * parity_a] += [plus + minus, middle]
                pending[2 * parity_a + 1].append(plus - minus)
            for index, cls in enumerate(CLASSES):
                held = sum(part.shape[0] for part in pending[index])
                final = q >= FINE_A_COUNT[cls[0]] - 1
                if pending[index] and (held % 16 == 0 or final):
                    if held % 16:
                        pending[index].append(jnp.zeros((8, columns), jnp.float32))
                        held += 8
                    store_split(
                        fine_pieces[index],
                        done[index],
                        class_fine_rows(cls),
                        jnp.concatenate(pending[index], 0),
                    )
                    done[index] += held
                    pending[index] = []
        for index in range(4):
            results[index] = multiply(backs[index], fine_pieces[index])
        for a in range(HALF):
            for plane, convected in zip((a, last - a), from_classes(results, a)):
                for c in range(LINE_POINT_TOTAL):
                    span = pl.ds((plane * 8 + c) * 8, 8)
                    mass = weight_b * float(weights[plane] * weights[c] / time_step)
                    gain_rhs[span, :] = gain[span, :] * (
                        mass * iterate[span, :] - fluid * convected[c * 8 : c * 8 + 8]
                    )
        for sweep_index in range(SWEEPS):
            if sweep_index > 0:
                to_classes(iterate, pieces)
            for index in range(4):
                results[index] = multiply(stiff[index], pieces[index])
            from_low = gain_low[...] * shifted(iterate[pl.ds(last * 64, 64), :], 1)
            from_high = gain_high[...] * shifted(iterate[pl.ds(0, 64), :], -1)
            wall = jnp.concatenate([iterate[pl.ds(a * 64, 8), :] for a in range(8)], 0)
            far = jnp.zeros_like(wall)
            for step in range(1, sections):
                far = jnp.where(distance == step, shifted(wall, -step * layout.slot), far)
            from_wall = gain_wall[...] * far
            for a in range(HALF):
                for plane, stiffness in zip((a, last - a), from_classes(results, a)):
                    span = pl.ds(plane * 64, 64)
                    value = (
                        keep[span, :] * iterate[span, :]
                        + gain_rhs[span, :]
                        - gain_k[span, :] * stiffness
                    )
                    if plane == 0:
                        value = value + from_low
                    if plane == last:
                        value = value + from_high
                    at_wall = value[:8] + from_wall[plane * 8 : plane * 8 + 8]
                    iterate[span, :] = jnp.concatenate([at_wall, value[8:]], 0)

    rows = layout.main_rows
    lane = lane_iota(rows)
    for section in range(sections):
        value = jnp.zeros((rows, LANES), jnp.float32)
        for group in range(sections):
            for tile, _, shift, first, last_lane in layout.window_pieces(
                section * layout.slot + GHOST, group * layout.main, layout.main
            ):
                block = iterate[pl.ds(group * rows, rows), pl.ds(tile * LANES, LANES)]
                value = jnp.where(in_range(lane, first, last_lane), turned(block, shift), value)
        outs[section][...] = value


def gather_kernel(layout, scalars, *refs):
    chunks, out = refs[: layout.sections], refs[layout.sections]
    here = scalars[0]
    rows, main, elements = layout.main_rows, layout.main, layout.elements
    lane = lane_iota(rows)
    places = [pair_of(here, shift, layout.sections) for shift in range(layout.sections)]
    for group in range(layout.sections):
        value = None
        for shift, there in enumerate(places):
            amount = lax.rem((there - group) * main + elements, elements)
            part = pltpu.roll(chunks[shift][...], amount, axis=1)
            value = (
                part
                if value is None
                else jnp.where(in_range(lane, there * main, (there + 1) * main), part, value)
            )
        for index in range(rows // 8):
            a, c = divmod(group * (rows // 8) + index, LINE_POINT_TOTAL)
            out[pl.ds(a * 64 + c, 8, stride=8), :] = value[index * 8 : index * 8 + 8]


def shape_of(*dims, dtype=jnp.float32):
    return jax.ShapeDtypeStruct(dims, dtype)


def in_vmem(count):
    return [pl.BlockSpec(memory_space=pltpu.VMEM)] * count


SCALAR = pl.BlockSpec(memory_space=pltpu.SMEM)
PARAMS = pltpu.CompilerParams(vmem_limit_bytes=48 * 1024 * 1024)


def body(
    thermal_level_points,
    flow_speed_vector,
    thermal_diffusivity_cell,
    metal_cell_indicator,
    adjoining_patch,
):
    sections = lax.axis_size("sec")
    blocks = lax.axis_size("elem")
    elements = thermal_diffusivity_cell.shape[1]
    layout = Layout(elements, sections)
    here = lax.axis_index("sec").astype(jnp.int32)
    scalars = here[None]
    position = lax.axis_index("elem") * elements + lax.iota(jnp.int32, elements)
    if sections & (sections - 1) == 0:
        relative = adjoining_patch[0] ^ here
    else:
        relative = (adjoining_patch[0] - here) % sections
    params = jnp.stack(
        [
            thermal_diffusivity_cell[0],
            metal_cell_indicator[0].astype(jnp.float32),
            relative.astype(jnp.float32),
            (position > 0).astype(jnp.float32),
            (position < elements * blocks - 1).astype(jnp.float32),
        ]
        + [jnp.zeros((elements,), jnp.float32)] * (PARAM_ROWS - 5),
        0,
    )
    temperature = thermal_level_points.reshape(POINTS, elements)
    velocity = flow_speed_vector.reshape(3, POINTS, elements)

    main_shape = shape_of(FIELDS * layout.main_rows + PARAM_ROWS, elements)
    ghost_shape = shape_of(FIELDS * layout.ghost_rows + PARAM_ROWS, elements)
    end_shape = shape_of(FIELDS * layout.end_rows + PARAM_ROWS, elements)
    packed = pl.pallas_call(
        functools.partial(pack_main_kernel, layout),
        out_shape=[main_shape] * sections + [end_shape] * 2 + [shape_of(FIELDS, POINTS, elements)],
        in_specs=[SCALAR] + in_vmem(3),
        out_specs=in_vmem(sections + 3),
        compiler_params=PARAMS,
        name="pack_main",
    )(scalars, temperature, velocity, params)
    mains, (low_end, high_end, ordered) = packed[:sections], packed[sections:]

    def swap(arrays):
        received = [arrays[0]]
        for shift in range(1, sections):
            pairs = [(i, pair_of(i, shift, sections)) for i in range(sections)]
            received.append(lax.ppermute(arrays[shift], "sec", pairs))
        if sections & (sections - 1):
            received[1:] = received[:0:-1]
        return received

    mains = swap(mains)
    forward = [(i, i + 1) for i in range(blocks - 1)]
    from_low = lax.ppermute(high_end, "elem", forward)
    from_high = lax.ppermute(low_end, "elem", [(i, j) for j, i in forward])
    ghosts = pl.pallas_call(
        functools.partial(pack_ghost_kernel, layout),
        out_shape=[ghost_shape] * sections,
        in_specs=[SCALAR] + in_vmem(4),
        out_specs=in_vmem(sections),
        scratch_shapes=[pltpu.VMEM((FIELDS, POINTS, elements), jnp.float32)],
        compiler_params=PARAMS,
        name="pack_ghost",
    )(scalars, ordered, params, from_low, from_high)
    ghosts = swap(ghosts)

    lifts, backs, stiff = make_matrices()
    columns = layout.columns
    matrices = [jnp.asarray(matrix) for matrix in lifts + backs + stiff]
    fine_rows = [class_fine_rows(cls) for cls in CLASSES]
    f32, bf16 = jnp.float32, jnp.bfloat16
    chunks = pl.pallas_call(
        functools.partial(main_kernel, layout, make_tables()),
        out_shape=[shape_of(layout.main_rows, elements)] * sections,
        in_specs=in_vmem(2 * sections + len(matrices)),
        out_specs=in_vmem(sections),
        scratch_shapes=[
            pltpu.VMEM((FIELDS, POINTS, columns), f32),
            pltpu.VMEM((PARAM_ROWS, columns), f32),
            *[pltpu.VMEM((rows, columns), f32) for _ in range(3) for rows in fine_rows],
            pltpu.VMEM((3, FINE, SLAB_ROWS, columns), f32),
            pltpu.VMEM((4, 2 * CLASS_ROWS, columns), bf16),
            pltpu.VMEM((4, CLASS_ROWS, columns), f32),
            *[pltpu.VMEM((POINTS, columns), f32) for _ in range(4)],
            *[pltpu.VMEM((64, columns), f32) for _ in range(3)],
            *[pltpu.VMEM((2 * rows, columns), bf16) for rows in fine_rows],
        ],
        compiler_params=PARAMS,
        name="march",
    )(*mains, *ghosts, *matrices)
    chunks = swap(chunks)
    result = pl.pallas_call(
        functools.partial(gather_kernel, layout),
        out_shape=shape_of(POINTS, elements),
        in_specs=[SCALAR] + in_vmem(sections),
        out_specs=pl.BlockSpec(memory_space=pltpu.VMEM),
        compiler_params=PARAMS,
        name="unpack",
    )(scalars, *chunks)
    return result.reshape(thermal_level_points.shape)


def solution(mesh):
    return jax.shard_map(
        body,
        mesh=mesh,
        in_specs=(
            P("sec", None, None, None, "elem"),
            P(None, "sec", None, None, None, "elem"),
            P("sec", "elem"),
            P("sec", "elem"),
            P("sec", "elem"),
        ),
        out_specs=P("sec", None, None, None, "elem"),
        check_vma=False,
    )
```

```python
import functools

import jax
import jax.numpy as jnp
import ml_dtypes
import numpy as np
from jax import lax
from jax.experimental import pallas as pl
from jax.experimental.pallas import tpu as pltpu
from jax.sharding import PartitionSpec as P

LINE_POINT_TOTAL = 8
FINE = 11
SWEEPS = 4
STEPS = 2
GHOST = STEPS * SWEEPS

time_step = 0.05
relaxation = 0.4
penalty = 30.0

POINTS = LINE_POINT_TOTAL**3
FIELDS = 4
PARTS = ((0, 1), (2, 3))
PARAM_ROWS = 8
LANES = 128
HALF = LINE_POINT_TOTAL // 2
MIRROR = FINE // 2
CLASSES = ((0, 0), (0, 1), (1, 0), (1, 1))
CLASS_ROWS = HALF * HALF * LINE_POINT_TOTAL


def round_up(value, unit):
    return -(-value // unit) * unit


PAIR_ROWS = round_up(MIRROR * FINE, 8)
MID_ROWS = round_up(FINE, 8)
SLAB_ROWS = 2 * PAIR_ROWS + MID_ROWS
FINE_C_ROWS = (PAIR_ROWS + MID_ROWS, PAIR_ROWS)
FINE_A_COUNT = (MIRROR + 1, MIRROR)


def class_fine_rows(cls):
    return round_up(FINE_A_COUNT[cls[0]] * FINE_C_ROWS[cls[1]], 16)


def legendre_pair(order, points):
    previous = points * 0.0 + 1.0
    current = points * 1.0
    for level in range(2, order + 1):
        previous, current = (
            current,
            ((2 * level - 1) * points * current - (level - 1) * previous) / level,
        )
    return (current, previous)


def make_tables():
    degree = LINE_POINT_TOTAL - 1
    gll_nodes = -np.cos(np.pi * np.arange(LINE_POINT_TOTAL) / degree)
    for repeat in range(100):
        current, previous = legendre_pair(degree, gll_nodes)
        gll_nodes = gll_nodes - (gll_nodes * current - previous) / (LINE_POINT_TOTAL * current)
    values, lower_values = legendre_pair(degree, gll_nodes)
    weights = 2.0 / (degree * (degree + 1) * values**2)
    spatial_derivative = np.zeros((LINE_POINT_TOTAL, LINE_POINT_TOTAL))
    for row_index in range(LINE_POINT_TOTAL):
        for column_index in range(LINE_POINT_TOTAL):
            if row_index != column_index:
                spatial_derivative[row_index, column_index] = values[row_index] / (
                    values[column_index] * (gll_nodes[row_index] - gll_nodes[column_index])
                )
    spatial_derivative[0, 0] = -degree * (degree + 1) / 4.0
    spatial_derivative[-1, -1] = degree * (degree + 1) / 4.0
    fine_nodes = -np.cos(np.pi * (np.arange(FINE) + 0.75) / (FINE + 0.5))
    for repeat in range(100):
        current, previous = legendre_pair(FINE, fine_nodes)
        slope = FINE * (fine_nodes * current - previous) / (fine_nodes * fine_nodes - 1.0)
        fine_nodes = fine_nodes - current / slope
    current, previous = legendre_pair(FINE, fine_nodes)
    slope = FINE * (fine_nodes * current - previous) / (fine_nodes * fine_nodes - 1.0)
    fine_weights = 2.0 / ((1.0 - fine_nodes * fine_nodes) * slope * slope)
    interpolation = np.ones((FINE, LINE_POINT_TOTAL))
    for column_index in range(LINE_POINT_TOTAL):
        for other_index in range(LINE_POINT_TOTAL):
            if other_index != column_index:
                interpolation[:, column_index] *= (fine_nodes - gll_nodes[other_index]) / (
                    gll_nodes[column_index] - gll_nodes[other_index]
                )
    stiffness_1d = spatial_derivative.T @ (weights[:, None] * spatial_derivative)
    return spatial_derivative, interpolation, stiffness_1d, weights, fine_weights


def parity_parts(matrix, out_rows, sign):
    near = matrix[:out_rows, :HALF]
    far = matrix[:out_rows, ::-1][:, :HALF]
    return (near + sign * far) * 0.5


def fine_matrix(cls, line_a, line_b, line_c):
    count_c = FINE_A_COUNT[cls[1]]
    full = np.einsum("xa,yc,zb->xyzacb", line_a, line_c, line_b)
    full = full.reshape(FINE_A_COUNT[cls[0]], count_c, FINE, CLASS_ROWS)
    slabs = np.zeros((FINE_A_COUNT[cls[0]], FINE_C_ROWS[cls[1]], CLASS_ROWS))
    slabs[:, : MIRROR * FINE] = full[:, :MIRROR].reshape(-1, MIRROR * FINE, CLASS_ROWS)
    if cls[1] == 0:
        slabs[:, PAIR_ROWS : PAIR_ROWS + FINE] = full[:, MIRROR]
    result = np.zeros((class_fine_rows(cls), CLASS_ROWS))
    result[: slabs.shape[0] * slabs.shape[1]] = slabs.reshape(-1, CLASS_ROWS)
    return result


def split_stack(matrix):
    high = matrix.astype(ml_dtypes.bfloat16)
    low = (matrix - high.astype(np.float64)).astype(ml_dtypes.bfloat16)
    return np.concatenate(
        [np.concatenate([high, high], 1), np.concatenate([low, low], 1)], 0
    )


def make_matrices():
    derivative, interpolation, stiffness, weights, fine_weights = make_tables()
    slope = interpolation @ derivative
    even = parity_parts(interpolation, MIRROR + 1, 1.0)
    odd = parity_parts(interpolation, MIRROR, -1.0)
    slope_even = parity_parts(slope, MIRROR + 1, -1.0)
    slope_odd = parity_parts(slope, MIRROR, 1.0)
    plain, steep = (even, odd), (slope_even, slope_odd)
    lifts = []
    for direction in (None, 0, 1, 2):
        for cls in CLASSES:
            line_a = (steep if direction == 0 else plain)[cls[0]]
            line_c = (steep if direction == 2 else plain)[cls[1]]
            line_b = slope if direction == 1 else interpolation
            lifts.append(split_stack(fine_matrix(cls, line_a, line_b, line_c)))
    backs = []
    for cls in CLASSES:
        lines = []
        for parity in cls:
            rows = FINE_A_COUNT[parity]
            lines.append(plain[parity] * fine_weights[:rows, None])
        backs.append(
            split_stack(
                fine_matrix(cls, lines[0], interpolation * fine_weights[:, None], lines[1]).T
            )
        )
    stiff = []
    for cls in CLASSES:
        parts = [
            parity_parts(stiffness, HALF, 1.0 - 2.0 * parity)[:HALF] for parity in cls
        ]
        mass = np.diag(weights[:HALF]) * 0.5
        total = (
            np.einsum("ij,kl,mn->ikmjln", parts[0], mass, np.diag(weights))
            + np.einsum("ij,kl,mn->ikmjln", mass, parts[1], np.diag(weights))
            + np.einsum("ij,kl,mn->ikmjln", mass, mass, stiffness)
        )
        stiff.append(split_stack(total.reshape(CLASS_ROWS, CLASS_ROWS)))
    return lifts, backs, stiff


class Layout:
    def __init__(self, elements, sections):
        assert sections & (sections - 1) == 0 and elements == LANES
        self.elements = elements
        self.sections = sections
        self.main = elements // sections
        self.unit = int(np.gcd(self.main, 2 * GHOST))
        assert self.unit in (GHOST, 2 * GHOST)
        self.slot = round_up(self.main + 2 * GHOST, max(self.unit, LANES // sections))
        self.columns = self.slot * sections
        self.tiles = self.columns // LANES
        self.main_rows = POINTS // sections
        self.units = elements // self.unit
        self.unit_rows = POINTS // self.units
        self.window_units = (self.main + 2 * GHOST) // self.unit
        self.region_units = (elements // 2 + 2 * GHOST) // self.unit
        self.half = sections // 2
        self.slot_units = self.slot // self.unit
        self.end_rows = POINTS // (elements // GHOST)

    def window_pieces(self, source, target, width):
        pieces = []
        done = 0
        while done < width:
            at, to = source + done, target + done
            step = min(width - done, LANES - at % LANES, LANES - to % LANES)
            first = to % LANES
            pieces.append((at // LANES, to // LANES, (to - at) % LANES, first, first + step))
            done += step
        return pieces


def lane_iota(rows):
    return lax.broadcasted_iota(jnp.int32, (rows, LANES), 1)


def in_range(lane, first, last):
    return (lane >= first) & (lane < last)


def turned(value, shift):
    if isinstance(shift, int) and shift % value.shape[-1] == 0:
        return value
    return pltpu.roll(value, shift % LANES if isinstance(shift, int) else shift, axis=1)


def exchange_groups(blocks, width):
    blocks = list(blocks)
    count = len(blocks)
    lane = lane_iota(next(block for block in blocks if block is not None).shape[0])
    step = 1
    while step < count:
        keep = (lane & (step * width)) == 0
        for index in range(count):
            if index & step:
                continue
            low, high = blocks[index], blocks[index | step]
            if low is None and high is None:
                continue
            zero = jnp.zeros(lane.shape, jnp.float32)
            up = zero if low is None else turned(low, -step * width)
            down = zero if high is None else turned(high, step * width)
            blocks[index] = jnp.where(keep, zero if low is None else low, down)
            blocks[index | step] = jnp.where(keep, up, zero if high is None else high)
        step *= 2
    return blocks


def pack_kernel(layout, blocks, scalars, *refs):
    inputs = refs[:5]
    outs, ends = refs[5 : 5 + 2 * len(PARTS)], refs[5 + 2 * len(PARTS) : 7 + 2 * len(PARTS)]
    held = refs[7 + 2 * len(PARTS) : 12 + 2 * len(PARTS)]
    packed, arrived = refs[12 + 2 * len(PARTS) :]
    temperature, velocity, conductivity, metal, patch = held
    elements, main, sections = layout.elements, layout.main, layout.sections
    unit, units, rows = layout.unit, layout.units, layout.unit_rows
    here, block = scalars[0], scalars[1]
    copies = [
        pltpu.make_async_copy(inputs[0], temperature, arrived.at[0]),
        *[
            pltpu.make_async_copy(inputs[1].at[d], velocity.at[d], arrived.at[1 + d])
            for d in range(3)
        ],
        *[
            pltpu.make_async_copy(inputs[i], held[i], arrived.at[2 + i]) for i in range(2, 5)
        ],
    ]
    for copy in copies:
        copy.start()
    for field in range(FIELDS):
        copies[field].wait()
        source = temperature if field == 0 else velocity.at[field - 1]
        groups = []
        for group in range(units):
            parts = []
            for index in range(group * rows // 8, (group + 1) * rows // 8):
                a, c = divmod(index, LINE_POINT_TOTAL)
                parts.append(source[pl.ds(a * 64 + c, 8, stride=8), :])
            groups.append(pltpu.roll(jnp.concatenate(parts, 0), GHOST, axis=1))
        for index, value in enumerate(exchange_groups(groups, unit)):
            packed[field, index] = value
    for copy in copies[FIELDS:]:
        copy.wait()
    position = block * elements + lax.broadcasted_iota(jnp.int32, (1, elements), 1)
    zero = jnp.zeros((1, elements), jnp.float32)
    params = jnp.concatenate(
        [
            conductivity[...],
            metal[...].astype(jnp.float32),
            (patch[...] ^ here).astype(jnp.float32),
            jnp.where(position > 0, 1.0, 0.0),
            jnp.where(position < elements * blocks - 1, 1.0, 0.0),
        ]
        + [zero] * (PARAM_ROWS - 5),
        0,
    )
    region = here // layout.half
    for part, part_fields in enumerate(PARTS):
        for side, there in enumerate((region, 1 - region)):
            out = outs[2 * part + side]
            row = 0
            for field in part_fields:
                for index in range(layout.region_units):
                    place = lax.rem(there * (units // 2) + index, units)
                    out[pl.ds(row, rows), :] = packed[field, place]
                    row += rows
            if part == 0:
                out[pl.ds(row, PARAM_ROWS), :] = pltpu.roll(
                    params, lax.rem(elements + GHOST - there * (elements // 2), elements), axis=1
                )
    swapped = here >= sections // 2
    lane = lane_iota(layout.end_rows)
    row = 0
    for field in range(FIELDS):
        if unit == GHOST:
            high, low = packed[field, 0], packed[field, 1]
        else:
            upper, lower = packed[field, 0, : rows // 2], packed[field, 0, rows // 2 :]
            keep = (lane & GHOST) == 0
            high = jnp.where(keep, upper, turned(lower, GHOST))
            low = jnp.where(keep, turned(upper, -GHOST), lower)
        ends[0][pl.ds(row, layout.end_rows), :] = jnp.where(swapped, low, high)
        ends[1][pl.ds(row, layout.end_rows), :] = jnp.where(swapped, high, low)
        row += layout.end_rows
    high = turned(params, GHOST)
    ends[0][pl.ds(row, PARAM_ROWS), :] = jnp.where(swapped, params, high)
    ends[1][pl.ds(row, PARAM_ROWS), :] = jnp.where(swapped, high, params)


def unpack_columns(layout, here, chunks, ends, fields, param_value):
    sections, unit, rows = layout.sections, layout.unit, layout.unit_rows
    end_rows = layout.end_rows
    within = lax.rem(here, layout.half)
    first_row = within * (layout.main // unit * rows)
    at_first, at_last = here == 0, here == sections - 1
    per_tile = LANES // unit
    end_lane = lane_iota(end_rows)

    def unit_block(field, section, index):
        part, place = next(
            (part, inside.index(field)) for part, inside in enumerate(PARTS) if field in inside
        )
        base = (place * layout.region_units + index) * rows
        block = chunks[part][section][pl.ds(pl.multiple_of(first_row + base, 8), rows), :]
        if index not in (0, layout.window_units - 1):
            return block
        replace = at_first if index == 0 else at_last
        end = ends[section][pl.ds(field * end_rows, end_rows), :]
        if unit == GHOST:
            return jnp.where(replace, end, block)
        if index == 0:
            parts = [end, turned(end, -GHOST)]
            mask = (end_lane & GHOST) == 0
        else:
            parts = [turned(end, GHOST), end]
            mask = (end_lane & GHOST) != 0
        mask = mask & replace
        return jnp.concatenate(
            [
                jnp.where(mask, part, block[i * end_rows : (i + 1) * end_rows])
                for i, part in enumerate(parts)
            ],
            0,
        )

    for field in range(FIELDS):
        for tile in range(layout.tiles):
            blocks = []
            for place in range(per_tile):
                section, index = divmod(tile * per_tile + place, layout.slot_units)
                inside = index < layout.window_units
                blocks.append(unit_block(field, section, index) if inside else None)
            for group, value in enumerate(exchange_groups(blocks, unit)):
                fields[field, pl.ds(group * rows, rows), pl.ds(tile * LANES, LANES)] = value

    lane = lane_iota(PARAM_ROWS)
    values = [jnp.zeros((PARAM_ROWS, LANES), jnp.float32) for _ in range(layout.tiles)]
    for section in range(sections):
        block = chunks[0][section][
            pl.ds(len(PARTS[0]) * layout.region_units * rows, PARAM_ROWS), :
        ]
        block = pltpu.roll(block, lax.rem(LANES - within * layout.main, LANES), axis=1)
        end = ends[section][pl.ds(FIELDS * end_rows, PARAM_ROWS), :]
        after = GHOST + layout.main
        block = jnp.where(at_first & (lane < GHOST), end, block)
        block = jnp.where(
            at_last & in_range(lane, after, after + GHOST), turned(end, after), block
        )
        for _, tile, shift, first, last in layout.window_pieces(
            0, section * layout.slot, after + GHOST
        ):
            values[tile] = jnp.where(in_range(lane, first, last), turned(block, shift), values[tile])
    for tile in range(layout.tiles):
        param_value[:, pl.ds(tile * LANES, LANES)] = values[tile]


def store_split(target, row, half, value):
    high = value.astype(jnp.bfloat16)
    target[pl.ds(row, value.shape[0]), :] = high
    target[pl.ds(half + row, value.shape[0]), :] = (value - high.astype(jnp.float32)).astype(
        jnp.bfloat16
    )


def to_classes(source, pieces):
    for a in range(HALF):
        near = source[pl.ds(a * 64, 64), :]
        far = source[pl.ds((LINE_POINT_TOTAL - 1 - a) * 64, 64), :]
        for parity_a, slab in enumerate((near + far, near - far)):
            lower = slab[: HALF * 8]
            upper = jnp.concatenate(
                [slab[(LINE_POINT_TOTAL - 1 - c) * 8 :][:8] for c in range(HALF)], 0
            )
            for parity_c, part in enumerate((lower + upper, lower - upper)):
                store_split(pieces[2 * parity_a + parity_c], a * HALF * 8, CLASS_ROWS, part)


def multiply(matrix, pieces):
    product = jnp.dot(matrix[...], pieces[...], preferred_element_type=jnp.float32)
    half = product.shape[0] // 2
    return product[:half] + product[half:]


def from_classes(results, a):
    span = pl.ds(a * HALF * 8, HALF * 8)
    ee, eo, oe, oo = [results[index, span, :] for index in range(4)]

    def along_c(even, odd):
        lower, upper = even + odd, even - odd
        return jnp.concatenate(
            [lower] + [upper[c * 8 : c * 8 + 8] for c in reversed(range(HALF))], 0
        )

    return along_c(ee + oe, eo + oo), along_c(ee - oe, eo - oo)


def fine_slabs(fine, q):
    halves = []
    for parity_a in range(2):
        if q >= FINE_A_COUNT[parity_a]:
            break
        even = fine[2 * parity_a][pl.ds(q * FINE_C_ROWS[0], FINE_C_ROWS[0]), :]
        odd = fine[2 * parity_a + 1][pl.ds(q * FINE_C_ROWS[1], FINE_C_ROWS[1]), :]
        halves.append((even[:PAIR_ROWS] + odd, even[:PAIR_ROWS] - odd, even[PAIR_ROWS:]))
    if len(halves) == 1:
        return [halves[0]]
    return [
        tuple(x + y for x, y in zip(*halves)),
        tuple(x - y for x, y in zip(*halves)),
    ]


def main_kernel(layout, tables, scalars, *refs):
    weights = tables[3]
    sections, columns = layout.sections, layout.columns
    here = scalars[0]
    refs = list(refs)

    def take(count):
        taken, refs[:] = refs[:count], refs[count:]
        return taken

    chunks, ends = [take(sections) for _ in PARTS], take(sections)
    stored = take(2)
    outs = take(sections)
    fields, param_value = take(2)
    fine = [take(4) for _ in range(3)]
    (lifted, point_pieces, results, keep, gain_rhs, gain_k, gain) = take(7)
    (gain_low, gain_high, gain_wall) = take(3)
    fine_pieces = take(4)
    matrices = take(2)
    (arrived,) = take(1)
    pieces = [point_pieces.at[index] for index in range(4)]
    heights = [2 * class_fine_rows(cls) for cls in CLASSES]
    starts = np.concatenate([[0], np.cumsum(heights * 4 + [2 * CLASS_ROWS] * 4)]).tolist()
    tall = [matrices[0].at[pl.ds(i, j - i)] for i, j in zip(starts[:-1], starts[1:])]
    lifts, stiff = tall[:16], tall[16:]
    wide = np.concatenate([[0], np.cumsum([round_up(h, LANES) for h in heights])]).tolist()
    backs = [matrices[1].at[:, pl.ds(i, h)] for i, h in zip(wide, heights)]
    copies = [
        pltpu.make_async_copy(
            stored[0].at[pl.ds(i, j - i)], matrices[0].at[pl.ds(i, j - i)], arrived.at[index]
        )
        for index, (i, j) in enumerate(zip(starts[0:17:4], starts[4:21:4]))
    ]
    copies.append(pltpu.make_async_copy(stored[1], matrices[1], arrived.at[5]))
    for copy in copies:
        copy.start()

    unpack_columns(layout, here, chunks, ends, fields, param_value)

    params = param_value[...]
    k, metal, partner, has_low, has_high = [params[row : row + 1] for row in range(5)]

    def shifted(value, amount):
        return pltpu.roll(value, amount % columns, axis=1)

    lane = lax.broadcasted_iota(jnp.int32, (1, columns), 1)
    own_slot = lane // layout.slot
    partner_slot = own_slot ^ partner.astype(jnp.int32)
    distance = lax.rem(partner_slot - own_slot + sections, sections)
    coef_low = has_low * (0.5 * penalty) * (k + shifted(k, 1))
    coef_high = has_high * (0.5 * penalty) * (k + shifted(k, -1))
    partner_k, partner_metal = jnp.zeros_like(k), jnp.zeros_like(k)
    for step in range(1, sections):
        chosen = distance == step
        partner_k = jnp.where(chosen, shifted(k, -step * layout.slot), partner_k)
        partner_metal = jnp.where(chosen, shifted(metal, -step * layout.slot), partner_metal)
    coef_wall = jnp.where(metal != partner_metal, (0.5 * penalty) * (k + partner_k), 0.0)
    fluid = 1.0 - metal

    row = lax.broadcasted_iota(jnp.int32, (8, columns), 0)
    weight_b = jnp.zeros((8, columns), jnp.float32)
    stiff_b = jnp.zeros((8, columns), jnp.float32)
    stiff_line = np.diagonal(tables[2])
    for b in range(8):
        weight_b = jnp.where(row == b, float(weights[b]), weight_b)
        stiff_b = jnp.where(row == b, float(stiff_line[b]), stiff_b)
    last = LINE_POINT_TOTAL - 1
    for a in range(LINE_POINT_TOTAL):
        for c in range(LINE_POINT_TOTAL):
            wa, wc = float(weights[a]), float(weights[c])
            mass = weight_b * (wa * wc / time_step)
            diag = mass + k * (
                weight_b * (float(stiff_line[a]) * wc + wa * float(stiff_line[c]))
                + stiff_b * (wa * wc)
            )
            face = None
            if a == 0:
                face_low = coef_low * (weight_b * wc)
                face = face_low
            if a == last:
                face_high = coef_high * (weight_b * wc)
                face = face_high
            if c == 0:
                face_wall = coef_wall * (weight_b * wa)
                face = face_wall if face is None else face + face_wall
            if face is not None:
                diag = diag + face
            factor = relaxation / diag
            span = pl.ds((a * 8 + c) * 8, 8)
            gain[span, :] = factor
            gain_k[span, :] = factor * k
            keep[span, :] = 1.0 - factor * (mass if face is None else mass + face)
            if a == 0:
                gain_low[pl.ds(c * 8, 8), :] = factor * face_low
            if a == last:
                gain_high[pl.ds(c * 8, 8), :] = factor * face_high
            if c == 0:
                gain_wall[pl.ds(a * 8, 8), :] = factor * face_wall

    for direction in range(3):
        to_classes(fields.at[direction + 1], pieces)
        if direction == 0:
            copies[0].wait()
        for index in range(4):
            fine[0][index][...] = multiply(lifts[index], pieces[index])
        for q in range(MIRROR + 1):
            for point, slab in zip((q, FINE - 1 - q), fine_slabs(fine[0], q)):
                base = 0
                for part in slab:
                    lifted[direction, point, pl.ds(base, part.shape[0]), :] = part
                    base += part.shape[0]

    for copy in copies[1:]:
        copy.wait()
    iterate = fields.at[0]
    for step_index in range(STEPS):
        to_classes(iterate, pieces)
        for direction in range(3):
            for index, cls in enumerate(CLASSES):
                source = index ^ (2 if direction == 0 else 1 if direction == 2 else 0)
                fine[direction][index][...] = multiply(
                    lifts[4 * (direction + 1) + index], pieces[source]
                )
        pending = [[], [], [], []]
        done = [0, 0, 0, 0]
        for q in range(MIRROR + 1):
            products = None
            for direction in range(3):
                slabs = fine_slabs(fine[direction], q)
                terms = []
                for point, slab in zip((q, FINE - 1 - q), slabs):
                    base = 0
                    parts = []
                    for part in slab:
                        parts.append(
                            part * lifted[direction, point, pl.ds(base, part.shape[0]), :]
                        )
                        base += part.shape[0]
                    terms.append(parts)
                products = (
                    terms
                    if products is None
                    else [[x + y for x, y in zip(s, t)] for s, t in zip(products, terms)]
                )
            if len(products) == 2:
                halves = [
                    [x + y for x, y in zip(*products)],
                    [x - y for x, y in zip(*products)],
                ]
            else:
                halves = products
            for parity_a, (plus, minus, middle) in enumerate(halves):
                pending[2 * parity_a] += [plus + minus, middle]
                pending[2 * parity_a + 1].append(plus - minus)
            for index, cls in enumerate(CLASSES):
                held = sum(part.shape[0] for part in pending[index])
                final = q >= FINE_A_COUNT[cls[0]] - 1
                if pending[index] and (held % 16 == 0 or final):
                    if held % 16:
                        pending[index].append(jnp.zeros((8, columns), jnp.float32))
                        held += 8
                    store_split(
                        fine_pieces[index],
                        done[index],
                        class_fine_rows(cls),
                        jnp.concatenate(pending[index], 0),
                    )
                    done[index] += held
                    pending[index] = []
        for index in range(4):
            results[index] = multiply(backs[index], fine_pieces[index])
        for a in range(HALF):
            for plane, convected in zip((a, last - a), from_classes(results, a)):
                for c in range(LINE_POINT_TOTAL):
                    span = pl.ds((plane * 8 + c) * 8, 8)
                    mass = weight_b * float(weights[plane] * weights[c] / time_step)
                    gain_rhs[span, :] = gain[span, :] * (
                        mass * iterate[span, :] - fluid * convected[c * 8 : c * 8 + 8]
                    )
        for sweep_index in range(SWEEPS):
            if sweep_index > 0:
                to_classes(iterate, pieces)
            for index in range(4):
                results[index] = multiply(stiff[index], pieces[index])
            from_low = gain_low[...] * shifted(iterate[pl.ds(last * 64, 64), :], 1)
            from_high = gain_high[...] * shifted(iterate[pl.ds(0, 64), :], -1)
            wall = jnp.concatenate([iterate[pl.ds(a * 64, 8), :] for a in range(8)], 0)
            far = jnp.zeros_like(wall)
            for step in range(1, sections):
                far = jnp.where(distance == step, shifted(wall, -step * layout.slot), far)
            from_wall = gain_wall[...] * far
            for a in range(HALF):
                for plane, stiffness in zip((a, last - a), from_classes(results, a)):
                    span = pl.ds(plane * 64, 64)
                    value = (
                        keep[span, :] * iterate[span, :]
                        + gain_rhs[span, :]
                        - gain_k[span, :] * stiffness
                    )
                    if plane == 0:
                        value = value + from_low
                    if plane == last:
                        value = value + from_high
                    at_wall = value[:8] + from_wall[plane * 8 : plane * 8 + 8]
                    iterate[span, :] = jnp.concatenate([at_wall, value[8:]], 0)

    rows = layout.main_rows
    lane = lane_iota(rows)
    for section in range(sections):
        value = jnp.zeros((rows, LANES), jnp.float32)
        for group in range(sections):
            for tile, _, shift, first, last_lane in layout.window_pieces(
                section * layout.slot + GHOST, group * layout.main, layout.main
            ):
                block = iterate[pl.ds(group * rows, rows), pl.ds(tile * LANES, LANES)]
                value = jnp.where(in_range(lane, first, last_lane), turned(block, shift), value)
        outs[section][...] = value


def gather_kernel(layout, scalars, *refs):
    chunks, out = refs[: layout.sections], refs[layout.sections]
    here = scalars[0]
    rows, main, elements = layout.main_rows, layout.main, layout.elements
    lane = lane_iota(rows)
    places = [here ^ shift for shift in range(layout.sections)]
    for group in range(layout.sections):
        value = None
        for shift, there in enumerate(places):
            amount = lax.rem((there - group) * main + elements, elements)
            part = pltpu.roll(chunks[shift][...], amount, axis=1)
            value = (
                part
                if value is None
                else jnp.where(in_range(lane, there * main, (there + 1) * main), part, value)
            )
        for index in range(rows // 8):
            a, c = divmod(group * (rows // 8) + index, LINE_POINT_TOTAL)
            out[pl.ds(a * 64 + c, 8, stride=8), :] = value[index * 8 : index * 8 + 8]


def shape_of(*dims, dtype=jnp.float32):
    return jax.ShapeDtypeStruct(dims, dtype)


def in_vmem(count):
    return [pl.BlockSpec(memory_space=pltpu.VMEM)] * count


def in_hbm(count):
    return [pl.BlockSpec(memory_space=pltpu.HBM)] * count


def kept_in_hbm(array):
    return pltpu.with_memory_space_constraint(array, pltpu.HBM)


SCALAR = pl.BlockSpec(memory_space=pltpu.SMEM)
PARAMS = pltpu.CompilerParams(vmem_limit_bytes=48 * 1024 * 1024)


def body(
    thermal_level_points,
    flow_speed_vector,
    thermal_diffusivity_cell,
    metal_cell_indicator,
    adjoining_patch,
):
    sections = lax.axis_size("sec")
    blocks = lax.axis_size("elem")
    elements = thermal_diffusivity_cell.shape[1]
    layout = Layout(elements, sections)
    scalars = jnp.stack([lax.axis_index("sec"), lax.axis_index("elem")]).astype(jnp.int32)
    f32, bf16 = jnp.float32, jnp.bfloat16
    dma = pltpu.SemaphoreType.DMA

    chunk_shapes = [
        shape_of(
            len(part) * layout.region_units * layout.unit_rows
            + (PARAM_ROWS if index == 0 else 0),
            elements,
        )
        for index, part in enumerate(PARTS)
        for _ in range(2)
    ]
    end_shape = shape_of(FIELDS * layout.end_rows + PARAM_ROWS, elements)
    packed = pl.pallas_call(
        functools.partial(pack_kernel, layout, blocks),
        out_shape=chunk_shapes + [end_shape] * 2,
        in_specs=[SCALAR] + in_hbm(5),
        out_specs=in_vmem(len(chunk_shapes) + 2),
        scratch_shapes=[
            pltpu.VMEM((POINTS, elements), f32),
            pltpu.VMEM((3, POINTS, elements), f32),
            pltpu.VMEM((1, elements), f32),
            pltpu.VMEM((1, elements), jnp.int32),
            pltpu.VMEM((1, elements), jnp.int32),
            pltpu.VMEM((FIELDS, layout.units, layout.unit_rows, elements), f32),
            dma((7,)),
        ],
        compiler_params=PARAMS,
        name="pack",
    )(
        scalars,
        *[
            kept_in_hbm(x)
            for x in (
                thermal_level_points.reshape(POINTS, elements),
                flow_speed_vector.reshape(3, POINTS, elements),
                thermal_diffusivity_cell,
                metal_cell_indicator,
                adjoining_patch,
            )
        ],
    )
    end_pair = packed[-2:]

    def across(array, mask):
        return lax.ppermute(array, "sec", [(i, i ^ mask) for i in range(sections)])

    chunks = [
        {0: packed[2 * part], layout.half: across(packed[2 * part + 1], layout.half)}
        for part in range(len(PARTS))
    ]
    ends = []
    for source in range(sections):
        mirrored = sections - 1 - source
        pairs = [(source * blocks + i, i + 1) for i in range(blocks - 1)]
        pairs += [
            (mirrored * blocks + i + 1, (sections - 1) * blocks + i) for i in range(blocks - 1)
        ]
        ends.append(
            lax.ppermute(end_pair[0 if source < sections // 2 else 1], ("sec", "elem"), pairs)
        )
    first, ends = lax.optimization_barrier((chunks[0][layout.half], ends))
    chunks[0][layout.half] = first
    for chunk in chunks:
        bit = layout.half // 2
        while bit:
            for mask in sorted(chunk):
                chunk[mask | bit] = across(chunk[mask], bit)
            bit //= 2
    chunks = [chunk[mask] for chunk in chunks for mask in range(sections)]
    lifts, backs, stiff = make_matrices()
    columns = layout.columns
    wide = [
        np.pad(matrix, ((0, 0), (0, round_up(matrix.shape[1], LANES) - matrix.shape[1])))
        for matrix in backs
    ]
    matrices = [
        jnp.asarray(np.concatenate(lifts + stiff, 0)),
        jnp.asarray(np.concatenate(wide, 1)),
    ]
    fine_rows = [class_fine_rows(cls) for cls in CLASSES]
    results = pl.pallas_call(
        functools.partial(main_kernel, layout, make_tables()),
        out_shape=[shape_of(layout.main_rows, elements)] * sections,
        in_specs=[SCALAR] + in_vmem(len(chunks) + sections) + in_hbm(len(matrices)),
        out_specs=in_vmem(sections),
        scratch_shapes=[
            pltpu.VMEM((FIELDS, POINTS, columns), f32),
            pltpu.VMEM((PARAM_ROWS, columns), f32),
            *[pltpu.VMEM((rows, columns), f32) for _ in range(3) for rows in fine_rows],
            pltpu.VMEM((3, FINE, SLAB_ROWS, columns), f32),
            pltpu.VMEM((4, 2 * CLASS_ROWS, columns), bf16),
            pltpu.VMEM((4, CLASS_ROWS, columns), f32),
            *[pltpu.VMEM((POINTS, columns), f32) for _ in range(4)],
            *[pltpu.VMEM((64, columns), f32) for _ in range(3)],
            *[pltpu.VMEM((2 * rows, columns), bf16) for rows in fine_rows],
            *[pltpu.VMEM(matrix.shape, bf16) for matrix in matrices],
            dma((6,)),
        ],
        compiler_params=PARAMS,
        name="march",
    )(scalars, *chunks, *ends, *[kept_in_hbm(matrix) for matrix in matrices])
    results = [results[0]] + [across(results[mask], mask) for mask in range(1, sections)]
    result = pl.pallas_call(
        functools.partial(gather_kernel, layout),
        out_shape=shape_of(POINTS, elements),
        in_specs=[SCALAR] + in_vmem(sections),
        out_specs=pl.BlockSpec(memory_space=pltpu.VMEM),
        compiler_params=PARAMS,
        name="unpack",
    )(scalars, *results)
    return result.reshape(thermal_level_points.shape)


def solution(mesh):
    return jax.shard_map(
        body,
        mesh=mesh,
        in_specs=(
            P("sec", None, None, None, "elem"),
            P(None, "sec", None, None, None, "elem"),
            P("sec", "elem"),
            P("sec", "elem"),
            P("sec", "elem"),
        ),
        out_specs=P("sec", None, None, None, "elem"),
        check_vma=False,
    )
```

```python
import functools

import jax
import jax.numpy as jnp
import ml_dtypes
import numpy as np
from jax import lax
from jax.experimental import pallas as pl
from jax.experimental.pallas import tpu as pltpu
from jax.sharding import PartitionSpec as P

LINE_POINT_TOTAL = 8
FINE = 11
SWEEPS = 4
STEPS = 2
GHOST = STEPS * SWEEPS

time_step = 0.05
relaxation = 0.4
penalty = 30.0

POINTS = LINE_POINT_TOTAL**3
FIELDS = 4
PARTS = ((0,), (1, 2, 3))
PARAM_ROWS = 8
LANES = 128
HALF = LINE_POINT_TOTAL // 2
MIRROR = FINE // 2
CLASSES = ((0, 0), (0, 1), (1, 0), (1, 1))
CLASS_ROWS = HALF * HALF * LINE_POINT_TOTAL


def round_up(value, unit):
    return -(-value // unit) * unit


PAIR_ROWS = round_up(MIRROR * FINE, 8)
MID_ROWS = round_up(FINE, 8)
SLAB_ROWS = 2 * PAIR_ROWS + MID_ROWS
FINE_C_ROWS = (PAIR_ROWS + MID_ROWS, PAIR_ROWS)
FINE_A_COUNT = (MIRROR + 1, MIRROR)


def class_fine_rows(cls):
    return round_up(FINE_A_COUNT[cls[0]] * FINE_C_ROWS[cls[1]], 16)


def legendre_pair(order, points):
    previous = points * 0.0 + 1.0
    current = points * 1.0
    for level in range(2, order + 1):
        previous, current = (
            current,
            ((2 * level - 1) * points * current - (level - 1) * previous) / level,
        )
    return (current, previous)


def make_tables():
    degree = LINE_POINT_TOTAL - 1
    gll_nodes = -np.cos(np.pi * np.arange(LINE_POINT_TOTAL) / degree)
    for repeat in range(100):
        current, previous = legendre_pair(degree, gll_nodes)
        gll_nodes = gll_nodes - (gll_nodes * current - previous) / (LINE_POINT_TOTAL * current)
    values, lower_values = legendre_pair(degree, gll_nodes)
    weights = 2.0 / (degree * (degree + 1) * values**2)
    spatial_derivative = np.zeros((LINE_POINT_TOTAL, LINE_POINT_TOTAL))
    for row_index in range(LINE_POINT_TOTAL):
        for column_index in range(LINE_POINT_TOTAL):
            if row_index != column_index:
                spatial_derivative[row_index, column_index] = values[row_index] / (
                    values[column_index] * (gll_nodes[row_index] - gll_nodes[column_index])
                )
    spatial_derivative[0, 0] = -degree * (degree + 1) / 4.0
    spatial_derivative[-1, -1] = degree * (degree + 1) / 4.0
    fine_nodes = -np.cos(np.pi * (np.arange(FINE) + 0.75) / (FINE + 0.5))
    for repeat in range(100):
        current, previous = legendre_pair(FINE, fine_nodes)
        slope = FINE * (fine_nodes * current - previous) / (fine_nodes * fine_nodes - 1.0)
        fine_nodes = fine_nodes - current / slope
    current, previous = legendre_pair(FINE, fine_nodes)
    slope = FINE * (fine_nodes * current - previous) / (fine_nodes * fine_nodes - 1.0)
    fine_weights = 2.0 / ((1.0 - fine_nodes * fine_nodes) * slope * slope)
    interpolation = np.ones((FINE, LINE_POINT_TOTAL))
    for column_index in range(LINE_POINT_TOTAL):
        for other_index in range(LINE_POINT_TOTAL):
            if other_index != column_index:
                interpolation[:, column_index] *= (fine_nodes - gll_nodes[other_index]) / (
                    gll_nodes[column_index] - gll_nodes[other_index]
                )
    stiffness_1d = spatial_derivative.T @ (weights[:, None] * spatial_derivative)
    return spatial_derivative, interpolation, stiffness_1d, weights, fine_weights


def parity_parts(matrix, out_rows, sign):
    near = matrix[:out_rows, :HALF]
    far = matrix[:out_rows, ::-1][:, :HALF]
    return (near + sign * far) * 0.5


def fine_matrix(cls, line_a, line_b, line_c):
    count_c = FINE_A_COUNT[cls[1]]
    full = np.einsum("xa,yc,zb->xyzacb", line_a, line_c, line_b)
    full = full.reshape(FINE_A_COUNT[cls[0]], count_c, FINE, CLASS_ROWS)
    slabs = np.zeros((FINE_A_COUNT[cls[0]], FINE_C_ROWS[cls[1]], CLASS_ROWS))
    slabs[:, : MIRROR * FINE] = full[:, :MIRROR].reshape(-1, MIRROR * FINE, CLASS_ROWS)
    if cls[1] == 0:
        slabs[:, PAIR_ROWS : PAIR_ROWS + FINE] = full[:, MIRROR]
    result = np.zeros((class_fine_rows(cls), CLASS_ROWS))
    result[: slabs.shape[0] * slabs.shape[1]] = slabs.reshape(-1, CLASS_ROWS)
    return result


def split_stack(matrix):
    high = matrix.astype(ml_dtypes.bfloat16)
    low = (matrix - high.astype(np.float64)).astype(ml_dtypes.bfloat16)
    return np.concatenate(
        [np.concatenate([high, high], 1), np.concatenate([low, low], 1)], 0
    )


def make_matrices():
    derivative, interpolation, stiffness, weights, fine_weights = make_tables()
    slope = interpolation @ derivative
    even = parity_parts(interpolation, MIRROR + 1, 1.0)
    odd = parity_parts(interpolation, MIRROR, -1.0)
    slope_even = parity_parts(slope, MIRROR + 1, -1.0)
    slope_odd = parity_parts(slope, MIRROR, 1.0)
    plain, steep = (even, odd), (slope_even, slope_odd)
    lifts = []
    for direction in (None, 0, 1, 2):
        for cls in CLASSES:
            line_a = (steep if direction == 0 else plain)[cls[0]]
            line_c = (steep if direction == 2 else plain)[cls[1]]
            line_b = slope if direction == 1 else interpolation
            lifts.append(split_stack(fine_matrix(cls, line_a, line_b, line_c)))
    backs = []
    for cls in CLASSES:
        lines = []
        for parity in cls:
            rows = FINE_A_COUNT[parity]
            lines.append(plain[parity] * fine_weights[:rows, None])
        backs.append(
            split_stack(
                fine_matrix(cls, lines[0], interpolation * fine_weights[:, None], lines[1]).T
            )
        )
    stiff = []
    for cls in CLASSES:
        parts = [
            parity_parts(stiffness, HALF, 1.0 - 2.0 * parity)[:HALF] for parity in cls
        ]
        mass = np.diag(weights[:HALF]) * 0.5
        total = (
            np.einsum("ij,kl,mn->ikmjln", parts[0], mass, np.diag(weights))
            + np.einsum("ij,kl,mn->ikmjln", mass, parts[1], np.diag(weights))
            + np.einsum("ij,kl,mn->ikmjln", mass, mass, stiffness)
        )
        stiff.append(split_stack(total.reshape(CLASS_ROWS, CLASS_ROWS)))
    return lifts, backs, stiff


class Layout:
    def __init__(self, elements, sections):
        assert sections & (sections - 1) == 0 and elements == LANES
        self.elements = elements
        self.sections = sections
        self.main = elements // sections
        self.unit = int(np.gcd(self.main, 2 * GHOST))
        assert self.unit in (GHOST, 2 * GHOST)
        self.slot = round_up(self.main + 2 * GHOST, max(self.unit, LANES // sections))
        self.columns = self.slot * sections
        self.tiles = self.columns // LANES
        self.main_rows = POINTS // sections
        self.units = elements // self.unit
        self.unit_rows = POINTS // self.units
        self.window_units = (self.main + 2 * GHOST) // self.unit
        self.slot_units = self.slot // self.unit
        self.end_rows = POINTS // (elements // GHOST)
        self.half = sections // 2
        self.whole_units = elements // 2 // self.unit
        self.tip_row = self.whole_units * self.unit_rows
        self.chunk_rows = self.tip_row + self.end_rows
        self.tips_rows = FIELDS * self.end_rows + PARAM_ROWS

    def window_pieces(self, source, target, width):
        pieces = []
        done = 0
        while done < width:
            at, to = source + done, target + done
            step = min(width - done, LANES - at % LANES, LANES - to % LANES)
            first = to % LANES
            pieces.append((at // LANES, to // LANES, (to - at) % LANES, first, first + step))
            done += step
        return pieces


def lane_iota(rows):
    return lax.broadcasted_iota(jnp.int32, (rows, LANES), 1)


def in_range(lane, first, last):
    return (lane >= first) & (lane < last)


def turned(value, shift):
    if isinstance(shift, int) and shift % value.shape[-1] == 0:
        return value
    return pltpu.roll(value, shift % LANES if isinstance(shift, int) else shift, axis=1)


def exchange_groups(blocks, width):
    blocks = list(blocks)
    count = len(blocks)
    lane = lane_iota(next(block for block in blocks if block is not None).shape[0])
    step = 1
    while step < count:
        keep = (lane & (step * width)) == 0
        for index in range(count):
            if index & step:
                continue
            low, high = blocks[index], blocks[index | step]
            if low is None and high is None:
                continue
            zero = jnp.zeros(lane.shape, jnp.float32)
            up = zero if low is None else turned(low, -step * width)
            down = zero if high is None else turned(high, step * width)
            blocks[index] = jnp.where(keep, zero if low is None else low, down)
            blocks[index | step] = jnp.where(keep, up, zero if high is None else high)
        step *= 2
    return blocks


def pack_field(layout, here, source, own, other, base, packed):
    unit, units, rows = layout.unit, layout.units, layout.unit_rows
    groups = []
    for group in range(units):
        parts = []
        for index in range(group * rows // 8, (group + 1) * rows // 8):
            a, c = divmod(index, LINE_POINT_TOTAL)
            parts.append(source[pl.ds(a * 64 + c, 8, stride=8), :])
        groups.append(pltpu.roll(jnp.concatenate(parts, 0), GHOST, axis=1))
    blocks = exchange_groups(groups, unit)
    for index, value in enumerate(blocks):
        packed[index] = value
    if unit == GHOST:
        high, low = blocks[0], blocks[1]
    else:
        upper, lower = blocks[0][: rows // 2], blocks[0][rows // 2 :]
        keep = (lane_iota(layout.end_rows) & GHOST) == 0
        high = jnp.where(keep, upper, turned(lower, GHOST))
        low = jnp.where(keep, turned(upper, -GHOST), lower)
    region = here // layout.half
    for out, there in ((own, region), (other, 1 - region)):
        first = jnp.where(there == 0, 2 * GHOST // unit, layout.whole_units)
        for index in range(layout.whole_units):
            out[pl.ds(base + index * rows, rows), :] = packed[first + index]
        out[pl.ds(base + layout.tip_row, layout.end_rows), :] = jnp.where(there == 0, low, high)
    return high, low


def pack_kernel(layout, blocks, scalars, *refs):
    inputs, outs, tips = refs[:5], refs[5 : 5 + 2 * len(PARTS)], refs[5 + 2 * len(PARTS)]
    *held, packed, arrived = refs[6 + 2 * len(PARTS) :]
    elements = layout.elements
    here, block = scalars[0], scalars[1]
    pairs = list(zip(inputs, held))
    pairs = pairs[:1] + [(x.at[d], y.at[d]) for x, y in pairs[1:2] for d in range(3)] + pairs[2:]
    copies = [
        pltpu.make_async_copy(source, target, arrived.at[index])
        for index, (source, target) in enumerate(pairs)
    ]
    for copy in copies:
        copy.start()
    rows = layout.end_rows
    for part, fields in enumerate(PARTS):
        for place, field in enumerate(fields):
            copies[field].wait()
            ends = pack_field(
                layout,
                here,
                pairs[field][1],
                outs[2 * part],
                outs[2 * part + 1],
                place * layout.chunk_rows,
                packed,
            )
            for index, end in enumerate(ends):
                tips[pl.ds(index * layout.tips_rows + field * rows, rows), :] = end
    for copy in copies[FIELDS:]:
        copy.wait()
    conductivity, metal, patch = held[2:]
    position = block * elements + lax.broadcasted_iota(jnp.int32, (1, elements), 1)
    zero = jnp.zeros((1, elements), jnp.float32)
    params = jnp.concatenate(
        [
            conductivity[...],
            metal[...].astype(jnp.float32),
            (patch[...] ^ here).astype(jnp.float32),
            jnp.where(position > 0, 1.0, 0.0),
            jnp.where(position < elements * blocks - 1, 1.0, 0.0),
        ]
        + [zero] * (PARAM_ROWS - 5),
        0,
    )
    region = here // layout.half
    for out, there in zip(outs[:2], (region, 1 - region)):
        out[pl.ds(len(PARTS[0]) * layout.chunk_rows, PARAM_ROWS), :] = pltpu.roll(
            params, lax.rem(elements + GHOST - there * (elements // 2), elements), axis=1
        )
    for index, param in enumerate((turned(params, GHOST), params)):
        tips[pl.ds((index + 1) * layout.tips_rows - PARAM_ROWS, PARAM_ROWS), :] = param


def join_kernel(layout, scalars, own, received, early, late):
    here = scalars[0]
    rows = layout.tips_rows
    is_even = lax.rem(here, 2) == 0
    lower = here < layout.half
    own_high, own_low = own[:rows, :], own[rows:, :]
    other_high, other_low = received[:rows, :], received[rows:, :]
    high = [jnp.where(is_even, own_high, other_high), jnp.where(is_even, other_high, own_high)]
    low = [jnp.where(is_even, other_low, own_low), jnp.where(is_even, own_low, other_low)]
    for index in range(2):
        early[pl.ds(index * rows, rows), :] = jnp.where(lower, high[index], low[index])
        late[pl.ds(index * rows, rows), :] = jnp.where(lower, low[index], high[index])


def tip_slice(layout, tips, section, first, rows):
    return tips[section // 2][pl.ds(section % 2 * layout.tips_rows + first, rows), :]


def unpack_field(layout, here, field, chunks, base, tips, target):
    sections, unit, rows = layout.sections, layout.unit, layout.unit_rows
    end_rows = layout.end_rows
    region, within = here // layout.half, lax.rem(here, layout.half)
    skipped = jnp.where(region == 0, 2 * GHOST // unit, 0)
    at_first, at_last = here == 0, here == sections - 1
    per_tile = LANES // unit
    final = layout.window_units - 1

    def merged(left, right):
        keep = (lane_iota(end_rows) & GHOST) == 0
        return jnp.concatenate(
            [
                jnp.where(keep, left, turned(right, GHOST)),
                jnp.where(keep, turned(left, -GHOST), right),
            ],
            0,
        )

    def unit_block(section, index):
        place = jnp.clip(
            within * (layout.main // unit) + index - skipped, 0, layout.whole_units - 1
        )
        block = chunks[section][pl.ds(pl.multiple_of(base + place * rows, 8), rows), :]
        inner = chunks[section][pl.ds(base + layout.tip_row, end_rows), :]
        outer = tip_slice(layout, tips, section, field * end_rows, end_rows)
        if unit == GHOST:
            if index == 0:
                block = jnp.where(at_first, outer, block)
            if index == 1:
                block = jnp.where(at_first, inner, block)
            if index == final - 1:
                block = jnp.where(at_last, inner, block)
            if index == final:
                block = jnp.where(at_last, outer, block)
            return block
        if index == 0:
            block = jnp.where(at_first, merged(outer, inner), block)
        if index == final:
            block = jnp.where(at_last, merged(inner, outer), block)
        return block

    for tile in range(layout.tiles):
        blocks = []
        for place in range(per_tile):
            section, index = divmod(tile * per_tile + place, layout.slot_units)
            blocks.append(unit_block(section, index) if index <= final else None)
        for group, value in enumerate(exchange_groups(blocks, unit)):
            target[pl.ds(group * rows, rows), pl.ds(tile * LANES, LANES)] = value


def unpack_params(layout, here, chunks, tips):
    sections = layout.sections
    within = lax.rem(here, layout.half)
    at_first, at_last = here == 0, here == sections - 1
    lane = lane_iota(PARAM_ROWS)
    after = GHOST + layout.main
    values = [jnp.zeros((PARAM_ROWS, LANES), jnp.float32) for _ in range(layout.tiles)]
    for section in range(sections):
        block = pltpu.roll(
            chunks[section][pl.ds(len(PARTS[0]) * layout.chunk_rows, PARAM_ROWS), :],
            lax.rem(LANES - within * layout.main, LANES),
            axis=1,
        )
        end = tip_slice(layout, tips, section, FIELDS * layout.end_rows, PARAM_ROWS)
        block = jnp.where(at_first & (lane < GHOST), end, block)
        block = jnp.where(
            at_last & in_range(lane, after, after + GHOST), turned(end, after), block
        )
        for _, tile, shift, first, last in layout.window_pieces(
            0, section * layout.slot, after + GHOST
        ):
            values[tile] = jnp.where(in_range(lane, first, last), turned(block, shift), values[tile])
    return jnp.concatenate(values, 1)


def store_split(target, row, half, value):
    high = value.astype(jnp.bfloat16)
    target[pl.ds(row, value.shape[0]), :] = high
    target[pl.ds(half + row, value.shape[0]), :] = (value - high.astype(jnp.float32)).astype(
        jnp.bfloat16
    )


def to_classes(source, pieces):
    for a in range(HALF):
        near = source[pl.ds(a * 64, 64), :]
        far = source[pl.ds((LINE_POINT_TOTAL - 1 - a) * 64, 64), :]
        for parity_a, slab in enumerate((near + far, near - far)):
            lower = slab[: HALF * 8]
            upper = jnp.concatenate(
                [slab[(LINE_POINT_TOTAL - 1 - c) * 8 :][:8] for c in range(HALF)], 0
            )
            for parity_c, part in enumerate((lower + upper, lower - upper)):
                store_split(pieces[2 * parity_a + parity_c], a * HALF * 8, CLASS_ROWS, part)


def multiply(matrix, pieces):
    product = jnp.dot(matrix[...], pieces[...], preferred_element_type=jnp.float32)
    half = product.shape[0] // 2
    return product[:half] + product[half:]


def from_classes(results, a):
    span = pl.ds(a * HALF * 8, HALF * 8)
    ee, eo, oe, oo = [results[index, span, :] for index in range(4)]

    def along_c(even, odd):
        lower, upper = even + odd, even - odd
        return jnp.concatenate(
            [lower] + [upper[c * 8 : c * 8 + 8] for c in reversed(range(HALF))], 0
        )

    return along_c(ee + oe, eo + oo), along_c(ee - oe, eo - oo)


def fine_slabs(fine, q):
    halves = []
    for parity_a in range(2):
        if q >= FINE_A_COUNT[parity_a]:
            break
        even = fine[2 * parity_a][pl.ds(q * FINE_C_ROWS[0], FINE_C_ROWS[0]), :]
        odd = fine[2 * parity_a + 1][pl.ds(q * FINE_C_ROWS[1], FINE_C_ROWS[1]), :]
        halves.append((even[:PAIR_ROWS] + odd, even[:PAIR_ROWS] - odd, even[PAIR_ROWS:]))
    if len(halves) == 1:
        return [halves[0]]
    return [
        tuple(x + y for x, y in zip(*halves)),
        tuple(x - y for x, y in zip(*halves)),
    ]


HEIGHTS = [2 * class_fine_rows(cls) for cls in CLASSES]
TALL = np.concatenate([[0], np.cumsum(HEIGHTS * 4 + [2 * CLASS_ROWS] * 4)]).tolist()
WIDE = np.concatenate([[0], np.cumsum([round_up(rows, LANES) for rows in HEIGHTS])]).tolist()


def lift_matrix(tall, direction, index):
    at = 4 * direction + index
    return tall.at[pl.ds(TALL[at], TALL[at + 1] - TALL[at])]


def shifted(value, amount):
    return pltpu.roll(value, amount % value.shape[1], axis=1)


def column_weights(line, columns):
    row = lax.broadcasted_iota(jnp.int32, (LINE_POINT_TOTAL, columns), 0)
    value = jnp.zeros((LINE_POINT_TOTAL, columns), jnp.float32)
    for b in range(LINE_POINT_TOTAL):
        value = jnp.where(row == b, float(line[b]), value)
    return value


def wall_distance(layout, params):
    lane = lax.broadcasted_iota(jnp.int32, (1, layout.columns), 1)
    own_slot = lane // layout.slot
    partner_slot = own_slot ^ params[2:3].astype(jnp.int32)
    return lax.rem(partner_slot - own_slot + layout.sections, layout.sections)


def store_slabs(fine, target):
    for q in range(MIRROR + 1):
        for point, slab in zip((q, FINE - 1 - q), fine_slabs(fine, q)):
            base = 0
            for part in slab:
                target[point, pl.ds(base, part.shape[0]), :] = part
                base += part.shape[0]


def gradients(tall, pieces, fine):
    for direction in range(3):
        for index in range(4):
            source = index ^ (2 if direction == 0 else 1 if direction == 2 else 0)
            fine[direction][index][...] = multiply(
                lift_matrix(tall, direction + 1, index), pieces[source]
            )


def start_kernel(layout, tables, scalars, *refs):
    sections, columns = layout.sections, layout.columns
    here = scalars[0]
    refs = list(refs)

    def take(count):
        taken, refs[:] = refs[:count], refs[count:]
        return taken

    chunks, tips, stored = take(sections), take(sections // 2), take(2)
    (iterate, param_value, keep, gain_k, gain, gain_low, gain_high, gain_wall) = take(8)
    slopes, (tall, wide) = take(3), take(2)
    fine, pieces, (arrived,) = take(4), take(4), take(1)
    copies = [
        pltpu.make_async_copy(
            stored[0].at[pl.ds(i, j - i)], tall.at[pl.ds(i, j - i)], arrived.at[index]
        )
        for index, (i, j) in enumerate(zip(TALL[0:17:4], TALL[4:21:4]))
    ]
    copies.append(pltpu.make_async_copy(stored[1], wide, arrived.at[5]))
    for index in (1, 2, 3, 0, 4, 5):
        copies[index].start()

    unpack_field(layout, here, 0, chunks, 0, tips, iterate)
    params = unpack_params(layout, here, chunks, tips)
    param_value[...] = params
    to_classes(iterate, pieces)
    for direction in range(3):
        copies[direction + 1].wait()
        for index in range(4):
            source = index ^ (2 if direction == 0 else 1 if direction == 2 else 0)
            fine[index][...] = multiply(lift_matrix(tall, direction + 1, index), pieces[source])
        store_slabs(fine, slopes[direction])

    weights, stiff_line = tables[3], np.diagonal(tables[2])
    k, metal, _, has_low, has_high = [params[row : row + 1] for row in range(5)]
    distance = wall_distance(layout, params)
    coef_low = has_low * (0.5 * penalty) * (k + shifted(k, 1))
    coef_high = has_high * (0.5 * penalty) * (k + shifted(k, -1))
    partner_k, partner_metal = jnp.zeros_like(k), jnp.zeros_like(k)
    for step in range(1, sections):
        chosen = distance == step
        partner_k = jnp.where(chosen, shifted(k, -step * layout.slot), partner_k)
        partner_metal = jnp.where(chosen, shifted(metal, -step * layout.slot), partner_metal)
    coef_wall = jnp.where(metal != partner_metal, (0.5 * penalty) * (k + partner_k), 0.0)
    weight_b = column_weights(weights, columns)
    stiff_b = column_weights(stiff_line, columns)
    last = LINE_POINT_TOTAL - 1
    for a in range(LINE_POINT_TOTAL):
        for c in range(LINE_POINT_TOTAL):
            wa, wc = float(weights[a]), float(weights[c])
            mass = weight_b * (wa * wc / time_step)
            diag = mass + k * (
                weight_b * (float(stiff_line[a]) * wc + wa * float(stiff_line[c]))
                + stiff_b * (wa * wc)
            )
            face = None
            if a == 0:
                face_low = coef_low * (weight_b * wc)
                face = face_low
            if a == last:
                face_high = coef_high * (weight_b * wc)
                face = face_high
            if c == 0:
                face_wall = coef_wall * (weight_b * wa)
                face = face_wall if face is None else face + face_wall
            if face is not None:
                diag = diag + face
            factor = relaxation / diag
            span = pl.ds((a * 8 + c) * 8, 8)
            gain[span, :] = factor
            gain_k[span, :] = factor * k
            keep[span, :] = 1.0 - factor * (mass if face is None else mass + face)
            if a == 0:
                gain_low[pl.ds(c * 8, 8), :] = factor * face_low
            if a == last:
                gain_high[pl.ds(c * 8, 8), :] = factor * face_high
            if c == 0:
                gain_wall[pl.ds(a * 8, 8), :] = factor * face_wall
    for index in (0, 4, 5):
        copies[index].wait()


def point_slabs(source, q):
    slabs = []
    for point in (q, FINE - 1 - q)[: 1 if q == MIRROR else 2]:
        slabs.append(
            [
                source[point, pl.ds(0, PAIR_ROWS), :],
                source[point, pl.ds(PAIR_ROWS, PAIR_ROWS), :],
                source[point, pl.ds(2 * PAIR_ROWS, MID_ROWS), :],
            ]
        )
    return slabs


def add_products(total, slabs, others):
    terms = [[x * y for x, y in zip(s, t)] for s, t in zip(slabs, others)]
    if total is None:
        return terms
    return [[x + y for x, y in zip(s, t)] for s, t in zip(total, terms)]


def project(layout, products_of, wide, fine_pieces, results):
    pending = [[], [], [], []]
    done = [0, 0, 0, 0]
    for q in range(MIRROR + 1):
        products = products_of(q)
        halves = products
        if len(products) == 2:
            halves = [
                [x + y for x, y in zip(*products)],
                [x - y for x, y in zip(*products)],
            ]
        for parity_a, (plus, minus, middle) in enumerate(halves):
            pending[2 * parity_a] += [plus + minus, middle]
            pending[2 * parity_a + 1].append(plus - minus)
        for index, cls in enumerate(CLASSES):
            held = sum(part.shape[0] for part in pending[index])
            final = q >= FINE_A_COUNT[cls[0]] - 1
            if pending[index] and (held % 16 == 0 or final):
                if held % 16:
                    pending[index].append(jnp.zeros((8, layout.columns), jnp.float32))
                    held += 8
                store_split(
                    fine_pieces[index],
                    done[index],
                    class_fine_rows(cls),
                    jnp.concatenate(pending[index], 0),
                )
                done[index] += held
                pending[index] = []
    for index in range(4):
        back = wide.at[:, pl.ds(WIDE[index], HEIGHTS[index])]
        results[index] = multiply(back, fine_pieces[index])


def march_kernel(layout, tables, scalars, *refs):
    weights = tables[3]
    sections, columns = layout.sections, layout.columns
    refs = list(refs)

    def take(count):
        taken, refs[:] = refs[:count], refs[count:]
        return taken

    chunks, tips = [take(sections) for _ in PARTS], take(sections // 2)
    (initial, param_value, keep, gain_k, gain, gain_low, gain_high, gain_wall) = take(8)
    slopes, (tall, wide) = take(3), take(2)
    outs = take(sections)
    (iterate, held, results, gain_rhs) = take(4)
    lifted = take(3)
    fine, pieces, fine_pieces = [take(4) for _ in range(3)], take(4), take(4)

    for d in range(3):
        part = next(index for index, inside in enumerate(PARTS) if 1 + d in inside)
        base = PARTS[part].index(1 + d) * layout.chunk_rows
        unpack_field(layout, scalars[0], 1 + d, chunks[part], base, tips, held)
        to_classes(held, pieces)
        for index in range(4):
            fine[0][index][...] = multiply(lift_matrix(tall, 0, index), pieces[index])
        store_slabs(fine[0], lifted[d])
    params = param_value[...]
    distance = wall_distance(layout, params)
    fluid = 1.0 - params[1:2]
    weight_b = column_weights(weights, columns)
    last = LINE_POINT_TOTAL - 1

    def first_products(q):
        total = None
        for slope, velocity in zip(slopes, lifted):
            total = add_products(total, point_slabs(slope, q), point_slabs(velocity, q))
        return total

    def later_products(q):
        total = None
        for slope, velocity in zip(fine, lifted):
            total = add_products(total, fine_slabs(slope, q), point_slabs(velocity, q))
        return total

    for step_index in range(STEPS):
        current = initial if step_index == 0 else iterate
        if step_index == 0:
            project(layout, first_products, wide, fine_pieces, results)
        else:
            to_classes(current, pieces)
            gradients(tall, pieces, fine)
            project(layout, later_products, wide, fine_pieces, results)
        for a in range(HALF):
            for plane, convected in zip((a, last - a), from_classes(results, a)):
                for c in range(LINE_POINT_TOTAL):
                    span = pl.ds((plane * 8 + c) * 8, 8)
                    mass = weight_b * float(weights[plane] * weights[c] / time_step)
                    gain_rhs[span, :] = gain[span, :] * (
                        mass * current[span, :] - fluid * convected[c * 8 : c * 8 + 8]
                    )
        for sweep_index in range(SWEEPS):
            current = initial if step_index == 0 and sweep_index == 0 else iterate
            if step_index == 0 or sweep_index > 0:
                to_classes(current, pieces)
            for index in range(4):
                stiff = tall.at[pl.ds(TALL[16 + index], 2 * CLASS_ROWS)]
                results[index] = multiply(stiff, pieces[index])
            from_low = gain_low[...] * shifted(current[pl.ds(last * 64, 64), :], 1)
            from_high = gain_high[...] * shifted(current[pl.ds(0, 64), :], -1)
            wall = jnp.concatenate([current[pl.ds(a * 64, 8), :] for a in range(8)], 0)
            far = jnp.zeros_like(wall)
            for step in range(1, sections):
                far = jnp.where(distance == step, shifted(wall, -step * layout.slot), far)
            from_wall = gain_wall[...] * far
            for a in range(HALF):
                for plane, stiffness in zip((a, last - a), from_classes(results, a)):
                    span = pl.ds(plane * 64, 64)
                    value = (
                        keep[span, :] * current[span, :]
                        + gain_rhs[span, :]
                        - gain_k[span, :] * stiffness
                    )
                    if plane == 0:
                        value = value + from_low
                    if plane == last:
                        value = value + from_high
                    at_wall = value[:8] + from_wall[plane * 8 : plane * 8 + 8]
                    iterate[span, :] = jnp.concatenate([at_wall, value[8:]], 0)

    rows = layout.main_rows
    lane = lane_iota(rows)
    for section in range(sections):
        value = jnp.zeros((rows, LANES), jnp.float32)
        for group in range(sections):
            for tile, _, shift, first, last_lane in layout.window_pieces(
                section * layout.slot + GHOST, group * layout.main, layout.main
            ):
                block = iterate[pl.ds(group * rows, rows), pl.ds(tile * LANES, LANES)]
                value = jnp.where(in_range(lane, first, last_lane), turned(block, shift), value)
        outs[section][...] = value


def gather_kernel(layout, scalars, *refs):
    chunks, (out, held, sent) = refs[: layout.sections], refs[layout.sections :]
    here = scalars[0]
    rows, main, elements = layout.main_rows, layout.main, layout.elements
    lane = lane_iota(rows)
    places = [here ^ shift for shift in range(layout.sections)]
    copies = []
    for group in range(layout.sections):
        value = None
        for shift, there in enumerate(places):
            amount = lax.rem((there - group) * main + elements, elements)
            part = pltpu.roll(chunks[shift][...], amount, axis=1)
            value = (
                part
                if value is None
                else jnp.where(in_range(lane, there * main, (there + 1) * main), part, value)
            )
        for index in range(rows // 8):
            a, c = divmod(group * (rows // 8) + index, LINE_POINT_TOTAL)
            held[pl.ds(a * 64 + c, 8, stride=8), :] = value[index * 8 : index * 8 + 8]
        planes = (group + 1) * rows // 64
        if planes > group * rows // 64:
            span = pl.ds((planes - max(1, rows // 64)) * 64, max(64, rows))
            copy = pltpu.make_async_copy(held.at[span], out.at[span], sent.at[group])
            copy.start()
            copies.append(copy)
    for copy in copies:
        copy.wait()


def shape_of(*dims, dtype=jnp.float32):
    return jax.ShapeDtypeStruct(dims, dtype)


def in_vmem(count):
    return [pl.BlockSpec(memory_space=pltpu.VMEM)] * count


def in_hbm(count):
    return [pl.BlockSpec(memory_space=pltpu.HBM)] * count


def kept_in_hbm(array):
    return pltpu.with_memory_space_constraint(array, pltpu.HBM)


FLOPS_BUSY = 1e8


SCALAR = pl.BlockSpec(memory_space=pltpu.SMEM)
PARAMS = pltpu.CompilerParams(vmem_limit_bytes=24 * 1024 * 1024)


def body(
    thermal_level_points,
    flow_speed_vector,
    thermal_diffusivity_cell,
    metal_cell_indicator,
    adjoining_patch,
):
    sections = lax.axis_size("sec")
    blocks = lax.axis_size("elem")
    elements = thermal_diffusivity_cell.shape[1]
    layout = Layout(elements, sections)
    scalars = jnp.stack([lax.axis_index("sec"), lax.axis_index("elem")]).astype(jnp.int32)
    f32, bf16 = jnp.float32, jnp.bfloat16
    dma = pltpu.SemaphoreType.DMA

    columns = layout.columns

    def call(kernel, name, out_shape, arrays, hbm=(), scratch=(), out_specs=None, busy=1.0):
        results = pl.pallas_call(
            kernel,
            out_shape=out_shape,
            in_specs=[SCALAR] + in_vmem(len(arrays)) + in_hbm(len(hbm)),
            out_specs=in_vmem(len(out_shape)) if out_specs is None else out_specs,
            scratch_shapes=list(scratch),
            compiler_params=PARAMS,
            cost_estimate=pl.CostEstimate(
                flops=int(busy * FLOPS_BUSY), bytes_accessed=0, transcendentals=0
            ),
            name=name,
        )(scalars, *arrays, *[kept_in_hbm(array) for array in hbm])
        return list(results)

    chunk_shapes = [
        shape_of(len(fields) * layout.chunk_rows + extra, elements)
        for fields, extra in zip(PARTS, (PARAM_ROWS, 0))
        for _ in range(2)
    ]
    *packed, tips = call(
        functools.partial(pack_kernel, layout, blocks),
        "pack",
        chunk_shapes + [shape_of(2 * layout.tips_rows, elements)],
        [],
        hbm=[
            thermal_level_points.reshape(POINTS, elements),
            flow_speed_vector.reshape(3, POINTS, elements),
            thermal_diffusivity_cell,
            metal_cell_indicator,
            adjoining_patch,
        ],
        scratch=[
            pltpu.VMEM((POINTS, elements), f32),
            pltpu.VMEM((3, POINTS, elements), f32),
            pltpu.VMEM((1, elements), f32),
            pltpu.VMEM((1, elements), jnp.int32),
            pltpu.VMEM((1, elements), jnp.int32),
            pltpu.VMEM((layout.units, layout.unit_rows, elements), f32),
            dma((7,)),
        ],
        busy=3.3,
    )

    def across(array, mask):
        return lax.ppermute(array, "sec", [(i, i ^ mask) for i in range(sections)])

    chunks = [
        {0: packed[2 * part], layout.half: across(packed[2 * part + 1], layout.half)}
        for part in range(len(PARTS))
    ]
    early, late = call(
        functools.partial(join_kernel, layout),
        "join",
        [shape_of(2 * layout.tips_rows, elements)] * 2,
        [tips, across(tips, 1)],
        busy=0.6,
    )
    tips = []
    for step in range(sections // 2):
        mirrored = sections // 2 - 1 - step
        up, down = 2 * step + 1, 2 * mirrored + 1
        pairs = [(up * blocks + i, i + 1) for i in range(blocks - 1)]
        pairs += [
            (down * blocks + i + 1, (sections - 1) * blocks + i) for i in range(blocks - 1)
        ]
        tips.append(
            lax.ppermute(early if step < sections // 4 else late, ("sec", "elem"), pairs)
        )
    def spread(chunk, after):
        chunk[layout.half], after = lax.optimization_barrier((chunk[layout.half], after))
        bit = layout.half // 2
        while bit:
            for mask in sorted(chunk):
                chunk[mask | bit] = across(chunk[mask], bit)
            bit //= 2
        return [chunk[mask] for mask in range(sections)], after

    chunks[0], tips = spread(chunks[0], tips)

    lifts, backs, stiff = make_matrices()
    tall = jnp.asarray(np.concatenate(lifts + stiff, 0))
    wide = jnp.asarray(
        np.concatenate(
            [
                np.pad(back, ((0, 0), (0, round_up(back.shape[1], LANES) - back.shape[1])))
                for back in backs
            ],
            1,
        )
    )
    tables = make_tables()
    fine_rows = [class_fine_rows(cls) for cls in CLASSES]
    points = shape_of(POINTS, columns)
    fine_field = shape_of(FINE, SLAB_ROWS, columns)
    face = shape_of(64, columns)
    fine_scratch = [pltpu.VMEM((rows, columns), f32) for rows in fine_rows]
    piece_scratch = [pltpu.VMEM((2 * CLASS_ROWS, columns), bf16) for _ in CLASSES]
    started = call(
        functools.partial(start_kernel, layout, tables),
        "start",
        [points, shape_of(PARAM_ROWS, columns)]
        + [points] * 3
        + [face] * 3
        + [fine_field] * 3
        + [shape_of(*tall.shape, dtype=bf16), shape_of(*wide.shape, dtype=bf16)],
        chunks[0] + tips,
        hbm=[tall, wide],
        scratch=fine_scratch + piece_scratch + [dma((6,))],
        busy=25.0,
    )
    factors, slopes, (tall, wide) = started[:8], started[8:11], started[11:]
    chunks[1], factors[1] = spread(chunks[1], factors[1])
    results = call(
        functools.partial(march_kernel, layout, tables),
        "march",
        [shape_of(layout.main_rows, elements)] * sections,
        chunks[0] + chunks[1] + tips + factors + slopes + [tall, wide],
        scratch=[
            pltpu.VMEM((POINTS, columns), f32),
            pltpu.VMEM((POINTS, columns), f32),
            pltpu.VMEM((4, CLASS_ROWS, columns), f32),
            pltpu.VMEM((POINTS, columns), f32),
            *[pltpu.VMEM((FINE, SLAB_ROWS, columns), f32) for _ in range(3)],
            *(fine_scratch * 3),
            *piece_scratch,
            *[pltpu.VMEM((2 * rows, columns), bf16) for rows in fine_rows],
        ],
        busy=8.9,
    )
    results = [results[0]] + [across(results[mask], mask) for mask in range(1, sections)]
    (result,) = call(
        functools.partial(gather_kernel, layout),
        "unpack",
        [shape_of(POINTS, elements)],
        list(results),
        scratch=[pltpu.VMEM((POINTS, elements), f32), dma((sections,))],
        out_specs=in_hbm(1),
        busy=1.5,
    )
    return result.reshape(thermal_level_points.shape)


def solution(mesh):
    return jax.shard_map(
        body,
        mesh=mesh,
        in_specs=(
            P("sec", None, None, None, "elem"),
            P(None, "sec", None, None, None, "elem"),
            P("sec", "elem"),
            P("sec", "elem"),
            P("sec", "elem"),
        ),
        out_specs=P("sec", None, None, None, "elem"),
        check_vma=False,
    )
```

```python
import functools

import jax
import jax.numpy as jnp
import ml_dtypes
import numpy as np
from jax import lax
from jax.experimental import pallas as pl
from jax.experimental.pallas import tpu as pltpu
from jax.sharding import PartitionSpec as P

LINE_POINT_TOTAL = 8
FINE = 11
SWEEPS = 4
STEPS = 2
GHOST = STEPS * SWEEPS

time_step = 0.05
relaxation = 0.4
penalty = 30.0

POINTS = LINE_POINT_TOTAL**3
FIELDS = 4
PARTS = ((0,), (1, 2, 3))
PARAM_ROWS = 8
LANES = 128
HALF = LINE_POINT_TOTAL // 2
MIRROR = FINE // 2
CLASSES = ((0, 0), (0, 1), (1, 0), (1, 1))
CLASS_ROWS = HALF * HALF * LINE_POINT_TOTAL


def round_up(value, unit):
    return -(-value // unit) * unit


PAIR_ROWS = round_up(MIRROR * FINE, 8)
MID_ROWS = round_up(FINE, 8)
SLAB_ROWS = 2 * PAIR_ROWS + MID_ROWS
FINE_C_ROWS = (PAIR_ROWS + MID_ROWS, PAIR_ROWS)
FINE_A_COUNT = (MIRROR + 1, MIRROR)


def class_fine_rows(cls):
    return round_up(FINE_A_COUNT[cls[0]] * FINE_C_ROWS[cls[1]], 16)


def legendre_pair(order, points):
    previous = points * 0.0 + 1.0
    current = points * 1.0
    for level in range(2, order + 1):
        previous, current = (
            current,
            ((2 * level - 1) * points * current - (level - 1) * previous) / level,
        )
    return (current, previous)


def make_tables():
    degree = LINE_POINT_TOTAL - 1
    gll_nodes = -np.cos(np.pi * np.arange(LINE_POINT_TOTAL) / degree)
    for repeat in range(100):
        current, previous = legendre_pair(degree, gll_nodes)
        gll_nodes = gll_nodes - (gll_nodes * current - previous) / (LINE_POINT_TOTAL * current)
    values, lower_values = legendre_pair(degree, gll_nodes)
    weights = 2.0 / (degree * (degree + 1) * values**2)
    spatial_derivative = np.zeros((LINE_POINT_TOTAL, LINE_POINT_TOTAL))
    for row_index in range(LINE_POINT_TOTAL):
        for column_index in range(LINE_POINT_TOTAL):
            if row_index != column_index:
                spatial_derivative[row_index, column_index] = values[row_index] / (
                    values[column_index] * (gll_nodes[row_index] - gll_nodes[column_index])
                )
    spatial_derivative[0, 0] = -degree * (degree + 1) / 4.0
    spatial_derivative[-1, -1] = degree * (degree + 1) / 4.0
    fine_nodes = -np.cos(np.pi * (np.arange(FINE) + 0.75) / (FINE + 0.5))
    for repeat in range(100):
        current, previous = legendre_pair(FINE, fine_nodes)
        slope = FINE * (fine_nodes * current - previous) / (fine_nodes * fine_nodes - 1.0)
        fine_nodes = fine_nodes - current / slope
    current, previous = legendre_pair(FINE, fine_nodes)
    slope = FINE * (fine_nodes * current - previous) / (fine_nodes * fine_nodes - 1.0)
    fine_weights = 2.0 / ((1.0 - fine_nodes * fine_nodes) * slope * slope)
    interpolation = np.ones((FINE, LINE_POINT_TOTAL))
    for column_index in range(LINE_POINT_TOTAL):
        for other_index in range(LINE_POINT_TOTAL):
            if other_index != column_index:
                interpolation[:, column_index] *= (fine_nodes - gll_nodes[other_index]) / (
                    gll_nodes[column_index] - gll_nodes[other_index]
                )
    stiffness_1d = spatial_derivative.T @ (weights[:, None] * spatial_derivative)
    return spatial_derivative, interpolation, stiffness_1d, weights, fine_weights


def parity_parts(matrix, out_rows, sign):
    near = matrix[:out_rows, :HALF]
    far = matrix[:out_rows, ::-1][:, :HALF]
    return (near + sign * far) * 0.5


def fine_matrix(cls, line_a, line_b, line_c):
    count_c = FINE_A_COUNT[cls[1]]
    full = np.einsum("xa,yc,zb->xyzacb", line_a, line_c, line_b)
    full = full.reshape(FINE_A_COUNT[cls[0]], count_c, FINE, CLASS_ROWS)
    slabs = np.zeros((FINE_A_COUNT[cls[0]], FINE_C_ROWS[cls[1]], CLASS_ROWS))
    slabs[:, : MIRROR * FINE] = full[:, :MIRROR].reshape(-1, MIRROR * FINE, CLASS_ROWS)
    if cls[1] == 0:
        slabs[:, PAIR_ROWS : PAIR_ROWS + FINE] = full[:, MIRROR]
    result = np.zeros((class_fine_rows(cls), CLASS_ROWS))
    result[: slabs.shape[0] * slabs.shape[1]] = slabs.reshape(-1, CLASS_ROWS)
    return result


def split_stack(matrix):
    high = matrix.astype(ml_dtypes.bfloat16)
    low = (matrix - high.astype(np.float64)).astype(ml_dtypes.bfloat16)
    return np.concatenate(
        [np.concatenate([high, high], 1), np.concatenate([low, low], 1)], 0
    )


def make_matrices():
    derivative, interpolation, stiffness, weights, fine_weights = make_tables()
    slope = interpolation @ derivative
    even = parity_parts(interpolation, MIRROR + 1, 1.0)
    odd = parity_parts(interpolation, MIRROR, -1.0)
    slope_even = parity_parts(slope, MIRROR + 1, -1.0)
    slope_odd = parity_parts(slope, MIRROR, 1.0)
    plain, steep = (even, odd), (slope_even, slope_odd)
    lifts = []
    for direction in (None, 0, 1, 2):
        for cls in CLASSES:
            line_a = (steep if direction == 0 else plain)[cls[0]]
            line_c = (steep if direction == 2 else plain)[cls[1]]
            line_b = slope if direction == 1 else interpolation
            lifts.append(split_stack(fine_matrix(cls, line_a, line_b, line_c)))
    backs = []
    for cls in CLASSES:
        lines = []
        for parity in cls:
            rows = FINE_A_COUNT[parity]
            lines.append(plain[parity] * fine_weights[:rows, None])
        backs.append(
            split_stack(
                fine_matrix(cls, lines[0], interpolation * fine_weights[:, None], lines[1]).T
            )
        )
    stiff = []
    for cls in CLASSES:
        parts = [
            parity_parts(stiffness, HALF, 1.0 - 2.0 * parity)[:HALF] for parity in cls
        ]
        mass = np.diag(weights[:HALF]) * 0.5
        total = (
            np.einsum("ij,kl,mn->ikmjln", parts[0], mass, np.diag(weights))
            + np.einsum("ij,kl,mn->ikmjln", mass, parts[1], np.diag(weights))
            + np.einsum("ij,kl,mn->ikmjln", mass, mass, stiffness)
        )
        stiff.append(split_stack(total.reshape(CLASS_ROWS, CLASS_ROWS)))
    return lifts, backs, stiff


class Layout:
    def __init__(self, elements, sections):
        assert sections & (sections - 1) == 0 and elements == LANES
        self.elements = elements
        self.sections = sections
        self.main = elements // sections
        self.unit = int(np.gcd(self.main, 2 * GHOST))
        assert self.unit in (GHOST, 2 * GHOST)
        self.slot = round_up(self.main + 2 * GHOST, max(self.unit, LANES // sections))
        self.columns = self.slot * sections
        self.tiles = self.columns // LANES
        self.main_rows = POINTS // sections
        self.units = elements // self.unit
        self.unit_rows = POINTS // self.units
        self.window_units = (self.main + 2 * GHOST) // self.unit
        self.slot_units = self.slot // self.unit
        self.end_rows = POINTS // (elements // GHOST)
        self.half = sections // 2
        self.whole_units = elements // 2 // self.unit
        self.tip_row = self.whole_units * self.unit_rows
        self.chunk_rows = self.tip_row + self.end_rows
        self.tips_rows = FIELDS * self.end_rows + PARAM_ROWS

    def window_pieces(self, source, target, width):
        pieces = []
        done = 0
        while done < width:
            at, to = source + done, target + done
            step = min(width - done, LANES - at % LANES, LANES - to % LANES)
            first = to % LANES
            pieces.append((at // LANES, to // LANES, (to - at) % LANES, first, first + step))
            done += step
        return pieces


def lane_iota(rows):
    return lax.broadcasted_iota(jnp.int32, (rows, LANES), 1)


def in_range(lane, first, last):
    return (lane >= first) & (lane < last)


def turned(value, shift):
    if isinstance(shift, int) and shift % value.shape[-1] == 0:
        return value
    return pltpu.roll(value, shift % LANES if isinstance(shift, int) else shift, axis=1)


def exchange_groups(blocks, width, offset=0):
    count = len(blocks)
    rows = next(block for block in blocks if block is not None).shape[0]
    lane = lane_iota(rows)
    zero = jnp.zeros((rows, LANES), jnp.float32)
    held = [
        zero if block is None else turned(block, index * width + offset)
        for index, block in enumerate(blocks)
    ]
    step = 1
    while step < count:
        stay = (lane & (step * width)) == 0
        held = [
            jnp.where(stay, held[index], held[(index + step) % count]) for index in range(count)
        ]
        step *= 2
    return [turned(held[-index % count], -index * width) for index in range(count)]


def pack_field(layout, here, source, own, other, base, packed):
    unit, units, rows = layout.unit, layout.units, layout.unit_rows
    groups = []
    for group in range(units):
        parts = []
        for index in range(group * rows // 8, (group + 1) * rows // 8):
            a, c = divmod(index, LINE_POINT_TOTAL)
            parts.append(source[pl.ds(a * 64 + c, 8, stride=8), :])
        groups.append(jnp.concatenate(parts, 0))
    blocks = exchange_groups(groups, unit, GHOST)
    for index, value in enumerate(blocks):
        packed[index] = value
    if unit == GHOST:
        high, low = blocks[0], blocks[1]
    else:
        upper, lower = blocks[0][: rows // 2], blocks[0][rows // 2 :]
        keep = (lane_iota(layout.end_rows) & GHOST) == 0
        high = jnp.where(keep, upper, turned(lower, GHOST))
        low = jnp.where(keep, turned(upper, -GHOST), lower)
    region = here // layout.half
    for out, there in ((own, region), (other, 1 - region)):
        first = jnp.where(there == 0, 2 * GHOST // unit, layout.whole_units)
        for index in range(layout.whole_units):
            out[pl.ds(base + index * rows, rows), :] = packed[first + index]
        out[pl.ds(base + layout.tip_row, layout.end_rows), :] = jnp.where(there == 0, low, high)
    return high, low


def pack_kernel(layout, blocks, scalars, *refs):
    inputs, outs, tips = refs[:5], refs[5 : 5 + 2 * len(PARTS)], refs[5 + 2 * len(PARTS)]
    *held, packed, arrived = refs[6 + 2 * len(PARTS) :]
    elements = layout.elements
    here, block = scalars[0], scalars[1]
    pairs = list(zip(inputs, held))
    pairs = pairs[:1] + [(x.at[d], y.at[d]) for x, y in pairs[1:2] for d in range(3)] + pairs[2:]
    copies = [
        pltpu.make_async_copy(source, target, arrived.at[index])
        for index, (source, target) in enumerate(pairs)
    ]
    for copy in copies:
        copy.start()
    rows = layout.end_rows
    for part, fields in enumerate(PARTS):
        for place, field in enumerate(fields):
            copies[field].wait()
            ends = pack_field(
                layout,
                here,
                pairs[field][1],
                outs[2 * part],
                outs[2 * part + 1],
                place * layout.chunk_rows,
                packed,
            )
            for index, end in enumerate(ends):
                tips[pl.ds(index * layout.tips_rows + field * rows, rows), :] = end
    for copy in copies[FIELDS:]:
        copy.wait()
    conductivity, metal, patch = held[2:]
    position = block * elements + lax.broadcasted_iota(jnp.int32, (1, elements), 1)
    zero = jnp.zeros((1, elements), jnp.float32)
    params = jnp.concatenate(
        [
            conductivity[...],
            metal[...].astype(jnp.float32),
            (patch[...] ^ here).astype(jnp.float32),
            jnp.where(position > 0, 1.0, 0.0),
            jnp.where(position < elements * blocks - 1, 1.0, 0.0),
        ]
        + [zero] * (PARAM_ROWS - 5),
        0,
    )
    region = here // layout.half
    for out, there in zip(outs[:2], (region, 1 - region)):
        out[pl.ds(len(PARTS[0]) * layout.chunk_rows, PARAM_ROWS), :] = pltpu.roll(
            params, lax.rem(elements + GHOST - there * (elements // 2), elements), axis=1
        )
    for index, param in enumerate((turned(params, GHOST), params)):
        tips[pl.ds((index + 1) * layout.tips_rows - PARAM_ROWS, PARAM_ROWS), :] = param


def join_kernel(layout, scalars, own, received, early, late):
    here = scalars[0]
    rows = layout.tips_rows
    is_even = lax.rem(here, 2) == 0
    lower = here < layout.half
    own_high, own_low = own[:rows, :], own[rows:, :]
    other_high, other_low = received[:rows, :], received[rows:, :]
    high = [jnp.where(is_even, own_high, other_high), jnp.where(is_even, other_high, own_high)]
    low = [jnp.where(is_even, other_low, own_low), jnp.where(is_even, own_low, other_low)]
    for index in range(2):
        early[pl.ds(index * rows, rows), :] = jnp.where(lower, high[index], low[index])
        late[pl.ds(index * rows, rows), :] = jnp.where(lower, low[index], high[index])


def tip_slice(layout, tips, section, first, rows):
    return tips[section // 2][pl.ds(section % 2 * layout.tips_rows + first, rows), :]


def unpack_field(layout, here, field, chunks, base, tips, target):
    sections, unit, rows = layout.sections, layout.unit, layout.unit_rows
    end_rows = layout.end_rows
    region, within = here // layout.half, lax.rem(here, layout.half)
    skipped = jnp.where(region == 0, 2 * GHOST // unit, 0)
    at_first, at_last = here == 0, here == sections - 1
    per_tile = LANES // unit
    final = layout.window_units - 1

    def merged(left, right):
        keep = (lane_iota(end_rows) & GHOST) == 0
        return jnp.concatenate(
            [
                jnp.where(keep, left, turned(right, GHOST)),
                jnp.where(keep, turned(left, -GHOST), right),
            ],
            0,
        )

    def unit_block(section, index):
        place = jnp.clip(
            within * (layout.main // unit) + index - skipped, 0, layout.whole_units - 1
        )
        block = chunks[section][pl.ds(pl.multiple_of(base + place * rows, 8), rows), :]
        inner = chunks[section][pl.ds(base + layout.tip_row, end_rows), :]
        outer = tip_slice(layout, tips, section, field * end_rows, end_rows)
        if unit == GHOST:
            if index == 0:
                block = jnp.where(at_first, outer, block)
            if index == 1:
                block = jnp.where(at_first, inner, block)
            if index == final - 1:
                block = jnp.where(at_last, inner, block)
            if index == final:
                block = jnp.where(at_last, outer, block)
            return block
        if index == 0:
            block = jnp.where(at_first, merged(outer, inner), block)
        if index == final:
            block = jnp.where(at_last, merged(inner, outer), block)
        return block

    for tile in range(layout.tiles):
        blocks = []
        for place in range(per_tile):
            section, index = divmod(tile * per_tile + place, layout.slot_units)
            blocks.append(unit_block(section, index) if index <= final else None)
        for group, value in enumerate(exchange_groups(blocks, unit)):
            target[pl.ds(group * rows, rows), pl.ds(tile * LANES, LANES)] = value


def unpack_params(layout, here, chunks, tips):
    sections = layout.sections
    within = lax.rem(here, layout.half)
    at_first, at_last = here == 0, here == sections - 1
    lane = lane_iota(PARAM_ROWS)
    after = GHOST + layout.main
    values = [jnp.zeros((PARAM_ROWS, LANES), jnp.float32) for _ in range(layout.tiles)]
    for section in range(sections):
        block = pltpu.roll(
            chunks[section][pl.ds(len(PARTS[0]) * layout.chunk_rows, PARAM_ROWS), :],
            lax.rem(LANES - within * layout.main, LANES),
            axis=1,
        )
        end = tip_slice(layout, tips, section, FIELDS * layout.end_rows, PARAM_ROWS)
        block = jnp.where(at_first & (lane < GHOST), end, block)
        block = jnp.where(
            at_last & in_range(lane, after, after + GHOST), turned(end, after), block
        )
        for _, tile, shift, first, last in layout.window_pieces(
            0, section * layout.slot, after + GHOST
        ):
            values[tile] = jnp.where(in_range(lane, first, last), turned(block, shift), values[tile])
    return jnp.concatenate(values, 1)


def store_split(target, row, half, value):
    high = value.astype(jnp.bfloat16)
    target[pl.ds(row, value.shape[0]), :] = high
    target[pl.ds(half + row, value.shape[0]), :] = (value - high.astype(jnp.float32)).astype(
        jnp.bfloat16
    )


def to_classes(source, pieces):
    for a in range(HALF):
        near = source[pl.ds(a * 64, 64), :]
        far = source[pl.ds((LINE_POINT_TOTAL - 1 - a) * 64, 64), :]
        for parity_a, slab in enumerate((near + far, near - far)):
            lower = slab[: HALF * 8]
            upper = jnp.concatenate(
                [slab[(LINE_POINT_TOTAL - 1 - c) * 8 :][:8] for c in range(HALF)], 0
            )
            for parity_c, part in enumerate((lower + upper, lower - upper)):
                store_split(pieces[2 * parity_a + parity_c], a * HALF * 8, CLASS_ROWS, part)


def multiply(matrix, pieces):
    product = jnp.dot(matrix[...], pieces[...], preferred_element_type=jnp.float32)
    half = product.shape[0] // 2
    return product[:half] + product[half:]


def from_classes(results, a):
    span = pl.ds(a * HALF * 8, HALF * 8)
    ee, eo, oe, oo = [results[index, span, :] for index in range(4)]

    def along_c(even, odd):
        lower, upper = even + odd, even - odd
        return jnp.concatenate(
            [lower] + [upper[c * 8 : c * 8 + 8] for c in reversed(range(HALF))], 0
        )

    return along_c(ee + oe, eo + oo), along_c(ee - oe, eo - oo)


def fine_slabs(fine, q):
    halves = []
    for parity_a in range(2):
        if q >= FINE_A_COUNT[parity_a]:
            break
        even = fine[2 * parity_a][pl.ds(q * FINE_C_ROWS[0], FINE_C_ROWS[0]), :]
        odd = fine[2 * parity_a + 1][pl.ds(q * FINE_C_ROWS[1], FINE_C_ROWS[1]), :]
        halves.append((even[:PAIR_ROWS] + odd, even[:PAIR_ROWS] - odd, even[PAIR_ROWS:]))
    if len(halves) == 1:
        return [halves[0]]
    return [
        tuple(x + y for x, y in zip(*halves)),
        tuple(x - y for x, y in zip(*halves)),
    ]


HEIGHTS = [2 * class_fine_rows(cls) for cls in CLASSES]
TALL = np.concatenate([[0], np.cumsum(HEIGHTS * 4 + [2 * CLASS_ROWS] * 4)]).tolist()
WIDE = np.concatenate([[0], np.cumsum([round_up(rows, LANES) for rows in HEIGHTS])]).tolist()


def lift_matrix(tall, direction, index):
    at = 4 * direction + index
    return tall.at[pl.ds(TALL[at], TALL[at + 1] - TALL[at])]


def shifted(value, amount):
    return pltpu.roll(value, amount % value.shape[1], axis=1)


def column_weights(line, columns):
    row = lax.broadcasted_iota(jnp.int32, (LINE_POINT_TOTAL, columns), 0)
    value = jnp.zeros((LINE_POINT_TOTAL, columns), jnp.float32)
    for b in range(LINE_POINT_TOTAL):
        value = jnp.where(row == b, float(line[b]), value)
    return value


def wall_distance(layout, params):
    lane = lax.broadcasted_iota(jnp.int32, (1, layout.columns), 1)
    own_slot = lane // layout.slot
    partner_slot = own_slot ^ params[2:3].astype(jnp.int32)
    return lax.rem(partner_slot - own_slot + layout.sections, layout.sections)


def store_slabs(fine, target):
    for q in range(MIRROR + 1):
        for point, slab in zip((q, FINE - 1 - q), fine_slabs(fine, q)):
            base = 0
            for part in slab:
                target[point, pl.ds(base, part.shape[0]), :] = part
                base += part.shape[0]


def gradients(tall, pieces, fine):
    for direction in range(3):
        for index in range(4):
            source = index ^ (2 if direction == 0 else 1 if direction == 2 else 0)
            fine[direction][index][...] = multiply(
                lift_matrix(tall, direction + 1, index), pieces[source]
            )


def start_kernel(layout, tables, scalars, *refs):
    sections, columns = layout.sections, layout.columns
    here = scalars[0]
    refs = list(refs)

    def take(count):
        taken, refs[:] = refs[:count], refs[count:]
        return taken

    chunks, tips = take(sections), take(sections // 2)
    (iterate, param_value, keep, gain_k, gain, gain_low, gain_high, gain_wall) = take(8)
    unpack_field(layout, here, 0, chunks, 0, tips, iterate)
    params = unpack_params(layout, here, chunks, tips)
    param_value[...] = params
    weights, stiff_line = tables[3], np.diagonal(tables[2])
    k, metal, _, has_low, has_high = [params[row : row + 1] for row in range(5)]
    distance = wall_distance(layout, params)
    coef_low = has_low * (0.5 * penalty) * (k + shifted(k, 1))
    coef_high = has_high * (0.5 * penalty) * (k + shifted(k, -1))
    partner_k, partner_metal = jnp.zeros_like(k), jnp.zeros_like(k)
    for step in range(1, sections):
        chosen = distance == step
        partner_k = jnp.where(chosen, shifted(k, -step * layout.slot), partner_k)
        partner_metal = jnp.where(chosen, shifted(metal, -step * layout.slot), partner_metal)
    coef_wall = jnp.where(metal != partner_metal, (0.5 * penalty) * (k + partner_k), 0.0)
    weight_b = column_weights(weights, columns)
    stiff_b = column_weights(stiff_line, columns)
    last = LINE_POINT_TOTAL - 1
    for a in range(LINE_POINT_TOTAL):
        for c in range(LINE_POINT_TOTAL):
            wa, wc = float(weights[a]), float(weights[c])
            mass = weight_b * (wa * wc / time_step)
            diag = mass + k * (
                weight_b * (float(stiff_line[a]) * wc + wa * float(stiff_line[c]))
                + stiff_b * (wa * wc)
            )
            face = None
            if a == 0:
                face_low = coef_low * (weight_b * wc)
                face = face_low
            if a == last:
                face_high = coef_high * (weight_b * wc)
                face = face_high
            if c == 0:
                face_wall = coef_wall * (weight_b * wa)
                face = face_wall if face is None else face + face_wall
            if face is not None:
                diag = diag + face
            factor = relaxation / diag
            span = pl.ds((a * 8 + c) * 8, 8)
            gain[span, :] = factor
            gain_k[span, :] = factor * k
            keep[span, :] = 1.0 - factor * (mass if face is None else mass + face)
            if a == 0:
                gain_low[pl.ds(c * 8, 8), :] = factor * face_low
            if a == last:
                gain_high[pl.ds(c * 8, 8), :] = factor * face_high
            if c == 0:
                gain_wall[pl.ds(a * 8, 8), :] = factor * face_wall


def slope_kernel(layout, scalars, *refs):
    (iterate, tall), slopes = refs[:2], refs[2:5]
    fine, pieces = [refs[5 + 4 * d : 9 + 4 * d] for d in range(3)], refs[17:21]
    to_classes(iterate, pieces)
    gradients(tall, pieces, fine)
    for direction in range(3):
        store_slabs(fine[direction], slopes[direction])


def point_slabs(source, q):
    slabs = []
    for point in (q, FINE - 1 - q)[: 1 if q == MIRROR else 2]:
        slabs.append(
            [
                source[point, pl.ds(0, PAIR_ROWS), :],
                source[point, pl.ds(PAIR_ROWS, PAIR_ROWS), :],
                source[point, pl.ds(2 * PAIR_ROWS, MID_ROWS), :],
            ]
        )
    return slabs


def add_products(total, slabs, others):
    terms = [[x * y for x, y in zip(s, t)] for s, t in zip(slabs, others)]
    if total is None:
        return terms
    return [[x + y for x, y in zip(s, t)] for s, t in zip(total, terms)]


def project(layout, products_of, wide, fine_pieces, results):
    pending = [[], [], [], []]
    done = [0, 0, 0, 0]
    for q in range(MIRROR + 1):
        products = products_of(q)
        halves = products
        if len(products) == 2:
            halves = [
                [x + y for x, y in zip(*products)],
                [x - y for x, y in zip(*products)],
            ]
        for parity_a, (plus, minus, middle) in enumerate(halves):
            pending[2 * parity_a] += [plus + minus, middle]
            pending[2 * parity_a + 1].append(plus - minus)
        for index, cls in enumerate(CLASSES):
            held = sum(part.shape[0] for part in pending[index])
            final = q >= FINE_A_COUNT[cls[0]] - 1
            if pending[index] and (held % 16 == 0 or final):
                if held % 16:
                    pending[index].append(jnp.zeros((8, layout.columns), jnp.float32))
                    held += 8
                store_split(
                    fine_pieces[index],
                    done[index],
                    class_fine_rows(cls),
                    jnp.concatenate(pending[index], 0),
                )
                done[index] += held
                pending[index] = []
    for index in range(4):
        back = wide.at[:, pl.ds(WIDE[index], HEIGHTS[index])]
        results[index] = multiply(back, fine_pieces[index])


def march_kernel(layout, tables, scalars, *refs):
    weights = tables[3]
    sections, columns = layout.sections, layout.columns
    refs = list(refs)

    def take(count):
        taken, refs[:] = refs[:count], refs[count:]
        return taken

    chunks, tips = [take(sections) for _ in PARTS], take(sections // 2)
    (initial, param_value, keep, gain_k, gain, gain_low, gain_high, gain_wall) = take(8)
    slopes, (tall, wide) = take(3), take(2)
    outs = take(sections)
    (iterate, held, results, gain_rhs) = take(4)
    lifted = take(3)
    fine, pieces, fine_pieces = [take(4) for _ in range(3)], take(4), take(4)

    for d in range(3):
        part = next(index for index, inside in enumerate(PARTS) if 1 + d in inside)
        base = PARTS[part].index(1 + d) * layout.chunk_rows
        unpack_field(layout, scalars[0], 1 + d, chunks[part], base, tips, held)
        to_classes(held, pieces)
        for index in range(4):
            fine[0][index][...] = multiply(lift_matrix(tall, 0, index), pieces[index])
        store_slabs(fine[0], lifted[d])
    params = param_value[...]
    distance = wall_distance(layout, params)
    fluid = 1.0 - params[1:2]
    weight_b = column_weights(weights, columns)
    last = LINE_POINT_TOTAL - 1

    def first_products(q):
        total = None
        for slope, velocity in zip(slopes, lifted):
            total = add_products(total, point_slabs(slope, q), point_slabs(velocity, q))
        return total

    def later_products(q):
        total = None
        for slope, velocity in zip(fine, lifted):
            total = add_products(total, fine_slabs(slope, q), point_slabs(velocity, q))
        return total

    for step_index in range(STEPS):
        current = initial if step_index == 0 else iterate
        if step_index == 0:
            project(layout, first_products, wide, fine_pieces, results)
        else:
            to_classes(current, pieces)
            gradients(tall, pieces, fine)
            project(layout, later_products, wide, fine_pieces, results)
        for a in range(HALF):
            for plane, convected in zip((a, last - a), from_classes(results, a)):
                for c in range(LINE_POINT_TOTAL):
                    span = pl.ds((plane * 8 + c) * 8, 8)
                    mass = weight_b * float(weights[plane] * weights[c] / time_step)
                    gain_rhs[span, :] = gain[span, :] * (
                        mass * current[span, :] - fluid * convected[c * 8 : c * 8 + 8]
                    )
        for sweep_index in range(SWEEPS):
            current = initial if step_index == 0 and sweep_index == 0 else iterate
            if step_index == 0 or sweep_index > 0:
                to_classes(current, pieces)
            for index in range(4):
                stiff = tall.at[pl.ds(TALL[16 + index], 2 * CLASS_ROWS)]
                results[index] = multiply(stiff, pieces[index])
            from_low = gain_low[...] * shifted(current[pl.ds(last * 64, 64), :], 1)
            from_high = gain_high[...] * shifted(current[pl.ds(0, 64), :], -1)
            wall = jnp.concatenate([current[pl.ds(a * 64, 8), :] for a in range(8)], 0)
            far = jnp.zeros_like(wall)
            for step in range(1, sections):
                far = jnp.where(distance == step, shifted(wall, -step * layout.slot), far)
            from_wall = gain_wall[...] * far
            for a in range(HALF):
                for plane, stiffness in zip((a, last - a), from_classes(results, a)):
                    span = pl.ds(plane * 64, 64)
                    value = (
                        keep[span, :] * current[span, :]
                        + gain_rhs[span, :]
                        - gain_k[span, :] * stiffness
                    )
                    if plane == 0:
                        value = value + from_low
                    if plane == last:
                        value = value + from_high
                    at_wall = value[:8] + from_wall[plane * 8 : plane * 8 + 8]
                    iterate[span, :] = jnp.concatenate([at_wall, value[8:]], 0)

    rows = layout.main_rows
    lane = lane_iota(rows)
    for section in range(sections):
        value = jnp.zeros((rows, LANES), jnp.float32)
        for group in range(sections):
            for tile, _, shift, first, last_lane in layout.window_pieces(
                section * layout.slot + GHOST, group * layout.main, layout.main
            ):
                block = iterate[pl.ds(group * rows, rows), pl.ds(tile * LANES, LANES)]
                value = jnp.where(in_range(lane, first, last_lane), turned(block, shift), value)
        outs[section][...] = value


def gather_kernel(layout, scalars, *refs):
    chunks, (out, held, sent) = refs[: layout.sections], refs[layout.sections :]
    here = scalars[0]
    rows, main, elements = layout.main_rows, layout.main, layout.elements
    lane = lane_iota(rows)
    sections = layout.sections
    held_chunks = [
        pltpu.roll(chunks[shift][...], lax.rem((here ^ shift) * main, elements), axis=1)
        for shift in range(sections)
    ]
    copies = []
    for group in range(sections):
        wanted = (lane // main + (sections - group)) % sections ^ here
        value = held_chunks[0]
        for shift in range(1, sections):
            value = jnp.where(wanted == shift, held_chunks[shift], value)
        value = turned(value, -group * main)
        for index in range(rows // 8):
            a, c = divmod(group * (rows // 8) + index, LINE_POINT_TOTAL)
            held[pl.ds(a * 64 + c, 8, stride=8), :] = value[index * 8 : index * 8 + 8]
        planes = (group + 1) * rows // 64
        if planes > group * rows // 64:
            span = pl.ds((planes - max(1, rows // 64)) * 64, max(64, rows))
            copy = pltpu.make_async_copy(held.at[span], out.at[span], sent.at[group])
            copy.start()
            copies.append(copy)
    for copy in copies:
        copy.wait()


def shape_of(*dims, dtype=jnp.float32):
    return jax.ShapeDtypeStruct(dims, dtype)


def in_vmem(count):
    return [pl.BlockSpec(memory_space=pltpu.VMEM)] * count


def in_hbm(count):
    return [pl.BlockSpec(memory_space=pltpu.HBM)] * count


def kept_in_hbm(array):
    return pltpu.with_memory_space_constraint(array, pltpu.HBM)


FLOPS_BUSY = 1e8


SCALAR = pl.BlockSpec(memory_space=pltpu.SMEM)
PARAMS = pltpu.CompilerParams(vmem_limit_bytes=24 * 1024 * 1024)


def body(
    thermal_level_points,
    flow_speed_vector,
    thermal_diffusivity_cell,
    metal_cell_indicator,
    adjoining_patch,
):
    sections = lax.axis_size("sec")
    blocks = lax.axis_size("elem")
    elements = thermal_diffusivity_cell.shape[1]
    layout = Layout(elements, sections)
    scalars = jnp.stack([lax.axis_index("sec"), lax.axis_index("elem")]).astype(jnp.int32)
    f32, bf16 = jnp.float32, jnp.bfloat16
    dma = pltpu.SemaphoreType.DMA

    columns = layout.columns

    def call(kernel, name, out_shape, arrays, hbm=(), scratch=(), out_specs=None, busy=1.0):
        results = pl.pallas_call(
            kernel,
            out_shape=out_shape,
            in_specs=[SCALAR] + in_vmem(len(arrays)) + in_hbm(len(hbm)),
            out_specs=in_vmem(len(out_shape)) if out_specs is None else out_specs,
            scratch_shapes=list(scratch),
            compiler_params=PARAMS,
            cost_estimate=pl.CostEstimate(
                flops=int(busy * FLOPS_BUSY), bytes_accessed=0, transcendentals=0
            ),
            name=name,
        )(scalars, *arrays, *[kept_in_hbm(array) for array in hbm])
        return list(results)

    chunk_shapes = [
        shape_of(len(fields) * layout.chunk_rows + extra, elements)
        for fields, extra in zip(PARTS, (PARAM_ROWS, 0))
        for _ in range(2)
    ]
    *packed, tips = call(
        functools.partial(pack_kernel, layout, blocks),
        "pack",
        chunk_shapes + [shape_of(2 * layout.tips_rows, elements)],
        [],
        hbm=[
            thermal_level_points.reshape(POINTS, elements),
            flow_speed_vector.reshape(3, POINTS, elements),
            thermal_diffusivity_cell,
            metal_cell_indicator,
            adjoining_patch,
        ],
        scratch=[
            pltpu.VMEM((POINTS, elements), f32),
            pltpu.VMEM((3, POINTS, elements), f32),
            pltpu.VMEM((1, elements), f32),
            pltpu.VMEM((1, elements), jnp.int32),
            pltpu.VMEM((1, elements), jnp.int32),
            pltpu.VMEM((layout.units, layout.unit_rows, elements), f32),
            dma((7,)),
        ],
        busy=3.3,
    )

    def across(array, mask):
        return lax.ppermute(array, "sec", [(i, i ^ mask) for i in range(sections)])

    chunks = [
        {0: packed[2 * part], layout.half: across(packed[2 * part + 1], layout.half)}
        for part in range(len(PARTS))
    ]
    early, late = call(
        functools.partial(join_kernel, layout),
        "join",
        [shape_of(2 * layout.tips_rows, elements)] * 2,
        [tips, across(tips, 1)],
        busy=0.6,
    )
    tips = []
    for step in range(sections // 2):
        mirrored = sections // 2 - 1 - step
        up, down = 2 * step + 1, 2 * mirrored + 1
        pairs = [(up * blocks + i, i + 1) for i in range(blocks - 1)]
        pairs += [
            (down * blocks + i + 1, (sections - 1) * blocks + i) for i in range(blocks - 1)
        ]
        tips.append(
            lax.ppermute(early if step < sections // 4 else late, ("sec", "elem"), pairs)
        )
    def spread(chunk, after):
        chunk[layout.half], after = lax.optimization_barrier((chunk[layout.half], after))
        bit = layout.half // 2
        while bit:
            for mask in sorted(chunk):
                chunk[mask | bit] = across(chunk[mask], bit)
            bit //= 2
        return [chunk[mask] for mask in range(sections)], after

    chunks[0], tips = spread(chunks[0], tips)

    lifts, backs, stiff = make_matrices()
    tall = jnp.asarray(np.concatenate(lifts + stiff, 0))
    wide = jnp.asarray(
        np.concatenate(
            [
                np.pad(back, ((0, 0), (0, round_up(back.shape[1], LANES) - back.shape[1])))
                for back in backs
            ],
            1,
        )
    )
    tables = make_tables()
    fine_rows = [class_fine_rows(cls) for cls in CLASSES]
    points = shape_of(POINTS, columns)
    fine_field = shape_of(FINE, SLAB_ROWS, columns)
    face = shape_of(64, columns)
    fine_scratch = [pltpu.VMEM((rows, columns), f32) for rows in fine_rows]
    piece_scratch = [pltpu.VMEM((2 * CLASS_ROWS, columns), bf16) for _ in CLASSES]
    started = call(
        functools.partial(start_kernel, layout, tables),
        "start",
        [points, shape_of(PARAM_ROWS, columns)]
        + [points] * 3
        + [face] * 3,
        chunks[0] + tips,
        busy=15.0,
    )
    factors = started
    slopes = call(
        functools.partial(slope_kernel, layout),
        "slope",
        [fine_field] * 3,
        [factors[0], tall],
        scratch=fine_scratch * 3 + piece_scratch,
        busy=15.0,
    )
    chunks[1], slopes[0] = spread(chunks[1], slopes[0])
    results = call(
        functools.partial(march_kernel, layout, tables),
        "march",
        [shape_of(layout.main_rows, elements)] * sections,
        chunks[0] + chunks[1] + tips + factors + slopes + [tall, wide],
        scratch=[
            pltpu.VMEM((POINTS, columns), f32),
            pltpu.VMEM((POINTS, columns), f32),
            pltpu.VMEM((4, CLASS_ROWS, columns), f32),
            pltpu.VMEM((POINTS, columns), f32),
            *[pltpu.VMEM((FINE, SLAB_ROWS, columns), f32) for _ in range(3)],
            *(fine_scratch * 3),
            *piece_scratch,
            *[pltpu.VMEM((2 * rows, columns), bf16) for rows in fine_rows],
        ],
        busy=8.9,
    )
    results = [results[0]] + [across(results[mask], mask) for mask in range(1, sections)]
    (result,) = call(
        functools.partial(gather_kernel, layout),
        "unpack",
        [shape_of(POINTS, elements)],
        list(results),
        scratch=[pltpu.VMEM((POINTS, elements), f32), dma((sections,))],
        out_specs=in_hbm(1),
        busy=1.5,
    )
    return result.reshape(thermal_level_points.shape)


def solution(mesh):
    return jax.shard_map(
        body,
        mesh=mesh,
        in_specs=(
            P("sec", None, None, None, "elem"),
            P(None, "sec", None, None, None, "elem"),
            P("sec", "elem"),
            P("sec", "elem"),
            P("sec", "elem"),
        ),
        out_specs=P("sec", None, None, None, "elem"),
        check_vma=False,
    )
```

```python
import functools

import jax
import jax.numpy as jnp
import ml_dtypes
import numpy as np
from jax import lax
from jax.experimental import pallas as pl
from jax.experimental.pallas import tpu as pltpu
from jax.sharding import PartitionSpec as P

LINE_POINT_TOTAL = 8
FINE = 11
SWEEPS = 4
STEPS = 2
GHOST = STEPS * SWEEPS

time_step = 0.05
relaxation = 0.4
penalty = 30.0

POINTS = LINE_POINT_TOTAL**3
FIELDS = 4
PARTS = ((0,), (1, 2, 3))
PARAM_ROWS = 8
LANES = 128
HALF = LINE_POINT_TOTAL // 2
MIRROR = FINE // 2
CLASSES = ((0, 0), (0, 1), (1, 0), (1, 1))
CLASS_ROWS = HALF * HALF * LINE_POINT_TOTAL


def round_up(value, unit):
    return -(-value // unit) * unit


PAIR_ROWS = round_up(MIRROR * FINE, 8)
MID_ROWS = round_up(FINE, 8)
SLAB_ROWS = 2 * PAIR_ROWS + MID_ROWS
FINE_C_ROWS = (PAIR_ROWS + MID_ROWS, PAIR_ROWS)
FINE_A_COUNT = (MIRROR + 1, MIRROR)


def class_fine_rows(cls):
    return round_up(FINE_A_COUNT[cls[0]] * FINE_C_ROWS[cls[1]], 16)


def legendre_pair(order, points):
    previous = points * 0.0 + 1.0
    current = points * 1.0
    for level in range(2, order + 1):
        previous, current = (
            current,
            ((2 * level - 1) * points * current - (level - 1) * previous) / level,
        )
    return (current, previous)


def make_tables():
    degree = LINE_POINT_TOTAL - 1
    gll_nodes = -np.cos(np.pi * np.arange(LINE_POINT_TOTAL) / degree)
    for repeat in range(100):
        current, previous = legendre_pair(degree, gll_nodes)
        gll_nodes = gll_nodes - (gll_nodes * current - previous) / (LINE_POINT_TOTAL * current)
    values, lower_values = legendre_pair(degree, gll_nodes)
    weights = 2.0 / (degree * (degree + 1) * values**2)
    spatial_derivative = np.zeros((LINE_POINT_TOTAL, LINE_POINT_TOTAL))
    for row_index in range(LINE_POINT_TOTAL):
        for column_index in range(LINE_POINT_TOTAL):
            if row_index != column_index:
                spatial_derivative[row_index, column_index] = values[row_index] / (
                    values[column_index] * (gll_nodes[row_index] - gll_nodes[column_index])
                )
    spatial_derivative[0, 0] = -degree * (degree + 1) / 4.0
    spatial_derivative[-1, -1] = degree * (degree + 1) / 4.0
    fine_nodes = -np.cos(np.pi * (np.arange(FINE) + 0.75) / (FINE + 0.5))
    for repeat in range(100):
        current, previous = legendre_pair(FINE, fine_nodes)
        slope = FINE * (fine_nodes * current - previous) / (fine_nodes * fine_nodes - 1.0)
        fine_nodes = fine_nodes - current / slope
    current, previous = legendre_pair(FINE, fine_nodes)
    slope = FINE * (fine_nodes * current - previous) / (fine_nodes * fine_nodes - 1.0)
    fine_weights = 2.0 / ((1.0 - fine_nodes * fine_nodes) * slope * slope)
    interpolation = np.ones((FINE, LINE_POINT_TOTAL))
    for column_index in range(LINE_POINT_TOTAL):
        for other_index in range(LINE_POINT_TOTAL):
            if other_index != column_index:
                interpolation[:, column_index] *= (fine_nodes - gll_nodes[other_index]) / (
                    gll_nodes[column_index] - gll_nodes[other_index]
                )
    stiffness_1d = spatial_derivative.T @ (weights[:, None] * spatial_derivative)
    return spatial_derivative, interpolation, stiffness_1d, weights, fine_weights


def parity_parts(matrix, out_rows, sign):
    near = matrix[:out_rows, :HALF]
    far = matrix[:out_rows, ::-1][:, :HALF]
    return (near + sign * far) * 0.5


def fine_matrix(cls, line_a, line_b, line_c):
    count_c = FINE_A_COUNT[cls[1]]
    full = np.einsum("xa,yc,zb->xyzacb", line_a, line_c, line_b)
    full = full.reshape(FINE_A_COUNT[cls[0]], count_c, FINE, CLASS_ROWS)
    slabs = np.zeros((FINE_A_COUNT[cls[0]], FINE_C_ROWS[cls[1]], CLASS_ROWS))
    slabs[:, : MIRROR * FINE] = full[:, :MIRROR].reshape(-1, MIRROR * FINE, CLASS_ROWS)
    if cls[1] == 0:
        slabs[:, PAIR_ROWS : PAIR_ROWS + FINE] = full[:, MIRROR]
    result = np.zeros((class_fine_rows(cls), CLASS_ROWS))
    result[: slabs.shape[0] * slabs.shape[1]] = slabs.reshape(-1, CLASS_ROWS)
    return result


def split_stack(matrix):
    high = matrix.astype(ml_dtypes.bfloat16)
    low = (matrix - high.astype(np.float64)).astype(ml_dtypes.bfloat16)
    return np.concatenate(
        [np.concatenate([high, high], 1), np.concatenate([low, low], 1)], 0
    )


def make_matrices():
    derivative, interpolation, stiffness, weights, fine_weights = make_tables()
    slope = interpolation @ derivative
    even = parity_parts(interpolation, MIRROR + 1, 1.0)
    odd = parity_parts(interpolation, MIRROR, -1.0)
    slope_even = parity_parts(slope, MIRROR + 1, -1.0)
    slope_odd = parity_parts(slope, MIRROR, 1.0)
    plain, steep = (even, odd), (slope_even, slope_odd)
    lifts = []
    for direction in (None, 0, 1, 2):
        for cls in CLASSES:
            line_a = (steep if direction == 0 else plain)[cls[0]]
            line_c = (steep if direction == 2 else plain)[cls[1]]
            line_b = slope if direction == 1 else interpolation
            lifts.append(split_stack(fine_matrix(cls, line_a, line_b, line_c)))
    backs = []
    for cls in CLASSES:
        lines = []
        for parity in cls:
            rows = FINE_A_COUNT[parity]
            lines.append(plain[parity] * fine_weights[:rows, None])
        backs.append(
            split_stack(
                fine_matrix(cls, lines[0], interpolation * fine_weights[:, None], lines[1]).T
            )
        )
    stiff = []
    for cls in CLASSES:
        parts = [
            parity_parts(stiffness, HALF, 1.0 - 2.0 * parity)[:HALF] for parity in cls
        ]
        mass = np.diag(weights[:HALF]) * 0.5
        total = (
            np.einsum("ij,kl,mn->ikmjln", parts[0], mass, np.diag(weights))
            + np.einsum("ij,kl,mn->ikmjln", mass, parts[1], np.diag(weights))
            + np.einsum("ij,kl,mn->ikmjln", mass, mass, stiffness)
        )
        stiff.append(split_stack(total.reshape(CLASS_ROWS, CLASS_ROWS)))
    return lifts, backs, stiff


class Layout:
    def __init__(self, elements, sections):
        assert sections & (sections - 1) == 0 and elements == LANES
        self.elements = elements
        self.sections = sections
        self.main = elements // sections
        self.unit = int(np.gcd(self.main, 2 * GHOST))
        assert self.unit in (GHOST, 2 * GHOST)
        self.slot = round_up(self.main + 2 * GHOST, max(self.unit, LANES // sections))
        self.columns = self.slot * sections
        self.tiles = self.columns // LANES
        self.main_rows = POINTS // sections
        self.units = elements // self.unit
        self.unit_rows = POINTS // self.units
        self.window_units = (self.main + 2 * GHOST) // self.unit
        self.slot_units = self.slot // self.unit
        self.end_rows = POINTS // (elements // GHOST)
        self.half = sections // 2
        self.whole_units = elements // 2 // self.unit
        self.tip_row = self.whole_units * self.unit_rows
        self.chunk_rows = self.tip_row + self.end_rows
        self.tips_rows = FIELDS * self.end_rows + PARAM_ROWS
        self.tips_base = len(PARTS[0]) * self.chunk_rows + PARAM_ROWS

    def window_pieces(self, source, target, width):
        pieces = []
        done = 0
        while done < width:
            at, to = source + done, target + done
            step = min(width - done, LANES - at % LANES, LANES - to % LANES)
            first = to % LANES
            pieces.append((at // LANES, to // LANES, (to - at) % LANES, first, first + step))
            done += step
        return pieces


def lane_iota(rows):
    return lax.broadcasted_iota(jnp.int32, (rows, LANES), 1)


def in_range(lane, first, last):
    return (lane >= first) & (lane < last)


def turned(value, shift):
    if isinstance(shift, int) and shift % value.shape[-1] == 0:
        return value
    return pltpu.roll(value, shift % LANES if isinstance(shift, int) else shift, axis=1)


def exchange_groups(blocks, width, offset=0):
    count = len(blocks)
    rows = next(block for block in blocks if block is not None).shape[0]
    lane = lane_iota(rows)
    zero = jnp.zeros((rows, LANES), jnp.float32)
    held = [
        zero if block is None else turned(block, index * width + offset)
        for index, block in enumerate(blocks)
    ]
    step = 1
    while step < count:
        stay = (lane & (step * width)) == 0
        held = [
            jnp.where(stay, held[index], held[(index + step) % count]) for index in range(count)
        ]
        step *= 2
    return [turned(held[-index % count], -index * width) for index in range(count)]


def pack_field(layout, here, source, own, other, base, packed):
    unit, units, rows = layout.unit, layout.units, layout.unit_rows
    groups = []
    for group in range(units):
        parts = []
        for index in range(group * rows // 8, (group + 1) * rows // 8):
            a, c = divmod(index, LINE_POINT_TOTAL)
            parts.append(source[pl.ds(a * 64 + c, 8, stride=8), :])
        groups.append(jnp.concatenate(parts, 0))
    blocks = exchange_groups(groups, unit, GHOST)
    for index, value in enumerate(blocks):
        packed[index] = value
    if unit == GHOST:
        high, low = blocks[0], blocks[1]
    else:
        upper, lower = blocks[0][: rows // 2], blocks[0][rows // 2 :]
        keep = (lane_iota(layout.end_rows) & GHOST) == 0
        high = jnp.where(keep, upper, turned(lower, GHOST))
        low = jnp.where(keep, turned(upper, -GHOST), lower)
    region = here // layout.half
    for out, there in ((own, region), (other, 1 - region)):
        first = jnp.where(there == 0, 2 * GHOST // unit, layout.whole_units)
        for index in range(layout.whole_units):
            out[pl.ds(base + index * rows, rows), :] = packed[first + index]
        out[pl.ds(base + layout.tip_row, layout.end_rows), :] = jnp.where(there == 0, low, high)
    return high, low


def pack_kernel(layout, blocks, scalars, *refs):
    inputs, outs = refs[:5], refs[5 : 5 + 2 * len(PARTS)]
    tips = outs[0].at[pl.ds(layout.tips_base, 2 * layout.tips_rows)]
    *held, packed, arrived = refs[5 + 2 * len(PARTS) :]
    elements = layout.elements
    here, block = scalars[0], scalars[1]
    pairs = list(zip(inputs, held))
    pairs = pairs[:1] + [(x.at[d], y.at[d]) for x, y in pairs[1:2] for d in range(3)] + pairs[2:]
    copies = [
        pltpu.make_async_copy(source, target, arrived.at[index])
        for index, (source, target) in enumerate(pairs)
    ]
    for copy in copies:
        copy.start()
    rows = layout.end_rows
    for part, fields in enumerate(PARTS):
        for place, field in enumerate(fields):
            copies[field].wait()
            ends = pack_field(
                layout,
                here,
                pairs[field][1],
                outs[2 * part],
                outs[2 * part + 1],
                place * layout.chunk_rows,
                packed,
            )
            for index, end in enumerate(ends):
                tips[pl.ds(index * layout.tips_rows + field * rows, rows), :] = end
    for copy in copies[FIELDS:]:
        copy.wait()
    conductivity, metal, patch = held[2:]
    position = block * elements + lax.broadcasted_iota(jnp.int32, (1, elements), 1)
    zero = jnp.zeros((1, elements), jnp.float32)
    params = jnp.concatenate(
        [
            conductivity[...],
            metal[...].astype(jnp.float32),
            (patch[...] ^ here).astype(jnp.float32),
            jnp.where(position > 0, 1.0, 0.0),
            jnp.where(position < elements * blocks - 1, 1.0, 0.0),
        ]
        + [zero] * (PARAM_ROWS - 5),
        0,
    )
    region = here // layout.half
    for out, there in zip(outs[:2], (region, 1 - region)):
        out[pl.ds(len(PARTS[0]) * layout.chunk_rows, PARAM_ROWS), :] = pltpu.roll(
            params, lax.rem(elements + GHOST - there * (elements // 2), elements), axis=1
        )
    for index, param in enumerate((turned(params, GHOST), params)):
        tips[pl.ds((index + 1) * layout.tips_rows - PARAM_ROWS, PARAM_ROWS), :] = param


def join_kernel(layout, scalars, own, received, early, late):
    here = scalars[0]
    rows, base = layout.tips_rows, layout.tips_base
    is_even = lax.rem(here, 2) == 0
    lower = here < layout.half
    own_high, own_low = [own[pl.ds(base + i * rows, rows), :] for i in range(2)]
    other_high, other_low = [received[pl.ds(base + i * rows, rows), :] for i in range(2)]
    high = [jnp.where(is_even, own_high, other_high), jnp.where(is_even, other_high, own_high)]
    low = [jnp.where(is_even, other_low, own_low), jnp.where(is_even, own_low, other_low)]
    for index in range(2):
        early[pl.ds(index * rows, rows), :] = jnp.where(lower, high[index], low[index])
        late[pl.ds(index * rows, rows), :] = jnp.where(lower, low[index], high[index])


def tip_slice(layout, tips, section, first, rows):
    return tips[section // 2][pl.ds(section % 2 * layout.tips_rows + first, rows), :]


def unpack_field(layout, here, field, chunks, base, tips, target):
    sections, unit, rows = layout.sections, layout.unit, layout.unit_rows
    end_rows = layout.end_rows
    region, within = here // layout.half, lax.rem(here, layout.half)
    skipped = jnp.where(region == 0, 2 * GHOST // unit, 0)
    at_first, at_last = here == 0, here == sections - 1
    per_tile = LANES // unit
    final = layout.window_units - 1

    def merged(left, right):
        keep = (lane_iota(end_rows) & GHOST) == 0
        return jnp.concatenate(
            [
                jnp.where(keep, left, turned(right, GHOST)),
                jnp.where(keep, turned(left, -GHOST), right),
            ],
            0,
        )

    def unit_block(section, index):
        place = jnp.clip(
            within * (layout.main // unit) + index - skipped, 0, layout.whole_units - 1
        )
        block = chunks[section][pl.ds(pl.multiple_of(base + place * rows, 8), rows), :]
        inner = chunks[section][pl.ds(base + layout.tip_row, end_rows), :]
        outer = tip_slice(layout, tips, section, field * end_rows, end_rows)
        if unit == GHOST:
            if index == 0:
                block = jnp.where(at_first, outer, block)
            if index == 1:
                block = jnp.where(at_first, inner, block)
            if index == final - 1:
                block = jnp.where(at_last, inner, block)
            if index == final:
                block = jnp.where(at_last, outer, block)
            return block
        if index == 0:
            block = jnp.where(at_first, merged(outer, inner), block)
        if index == final:
            block = jnp.where(at_last, merged(inner, outer), block)
        return block

    by_tile = []
    for tile in range(layout.tiles):
        blocks = []
        for place in range(per_tile):
            section, index = divmod(tile * per_tile + place, layout.slot_units)
            blocks.append(unit_block(section, index) if index <= final else None)
        by_tile.append(exchange_groups(blocks, unit))
    groups = [jnp.concatenate(values, 1) for values in zip(*by_tile)]
    joined = 64 // rows
    planes = [
        jnp.concatenate(groups[a * joined : (a + 1) * joined], 0) for a in range(LINE_POINT_TOTAL)
    ]
    if target is not None:
        for a, plane in enumerate(planes):
            target[pl.ds(a * 64, 64), :] = plane
    return planes


def unpack_params(layout, here, chunks, tips):
    sections = layout.sections
    within = lax.rem(here, layout.half)
    at_first, at_last = here == 0, here == sections - 1
    lane = lane_iota(PARAM_ROWS)
    after = GHOST + layout.main
    values = [jnp.zeros((PARAM_ROWS, LANES), jnp.float32) for _ in range(layout.tiles)]
    for section in range(sections):
        block = pltpu.roll(
            chunks[section][pl.ds(len(PARTS[0]) * layout.chunk_rows, PARAM_ROWS), :],
            lax.rem(LANES - within * layout.main, LANES),
            axis=1,
        )
        end = tip_slice(layout, tips, section, FIELDS * layout.end_rows, PARAM_ROWS)
        block = jnp.where(at_first & (lane < GHOST), end, block)
        block = jnp.where(
            at_last & in_range(lane, after, after + GHOST), turned(end, after), block
        )
        for _, tile, shift, first, last in layout.window_pieces(
            0, section * layout.slot, after + GHOST
        ):
            values[tile] = jnp.where(in_range(lane, first, last), turned(block, shift), values[tile])
    return jnp.concatenate(values, 1)


def store_split(target, row, half, value):
    high = value.astype(jnp.bfloat16)
    target[pl.ds(row, value.shape[0]), :] = high
    target[pl.ds(half + row, value.shape[0]), :] = (value - high.astype(jnp.float32)).astype(
        jnp.bfloat16
    )


def to_classes(source, pieces):
    planes = source
    if not isinstance(source, list):
        planes = [source[pl.ds(a * 64, 64), :] for a in range(LINE_POINT_TOTAL)]
    for a in range(HALF):
        near, far = planes[a], planes[LINE_POINT_TOTAL - 1 - a]
        for parity_a, slab in enumerate((near + far, near - far)):
            lower = slab[: HALF * 8]
            upper = jnp.concatenate(
                [slab[(LINE_POINT_TOTAL - 1 - c) * 8 :][:8] for c in range(HALF)], 0
            )
            for parity_c, part in enumerate((lower + upper, lower - upper)):
                store_split(pieces[2 * parity_a + parity_c], a * HALF * 8, CLASS_ROWS, part)


def multiply(matrix, pieces):
    product = jnp.dot(matrix[...], pieces[...], preferred_element_type=jnp.float32)
    half = product.shape[0] // 2
    return product[:half] + product[half:]


def from_classes(results, a):
    span = pl.ds(a * HALF * 8, HALF * 8)
    ee, eo, oe, oo = [results[index, span, :] for index in range(4)]

    def along_c(even, odd):
        lower, upper = even + odd, even - odd
        return jnp.concatenate(
            [lower] + [upper[c * 8 : c * 8 + 8] for c in reversed(range(HALF))], 0
        )

    return along_c(ee + oe, eo + oo), along_c(ee - oe, eo - oo)


def fine_slabs(fine, q):
    halves = []
    for parity_a in range(2):
        if q >= FINE_A_COUNT[parity_a]:
            break
        even = fine[2 * parity_a][pl.ds(q * FINE_C_ROWS[0], FINE_C_ROWS[0]), :]
        odd = fine[2 * parity_a + 1][pl.ds(q * FINE_C_ROWS[1], FINE_C_ROWS[1]), :]
        halves.append((even[:PAIR_ROWS] + odd, even[:PAIR_ROWS] - odd, even[PAIR_ROWS:]))
    if len(halves) == 1:
        return [halves[0]]
    return [
        tuple(x + y for x, y in zip(*halves)),
        tuple(x - y for x, y in zip(*halves)),
    ]


HEIGHTS = [2 * class_fine_rows(cls) for cls in CLASSES]
TALL = np.concatenate([[0], np.cumsum(HEIGHTS * 4 + [2 * CLASS_ROWS] * 4)]).tolist()
WIDE = np.concatenate([[0], np.cumsum([round_up(rows, LANES) for rows in HEIGHTS])]).tolist()


def lift_matrix(tall, direction, index):
    at = 4 * direction + index
    return tall.at[pl.ds(TALL[at], TALL[at + 1] - TALL[at])]


def shifted(value, amount):
    return pltpu.roll(value, amount % value.shape[1], axis=1)


def column_weights(line, columns):
    row = lax.broadcasted_iota(jnp.int32, (LINE_POINT_TOTAL, columns), 0)
    value = jnp.zeros((LINE_POINT_TOTAL, columns), jnp.float32)
    for b in range(LINE_POINT_TOTAL):
        value = jnp.where(row == b, float(line[b]), value)
    return value


def wall_distance(layout, params):
    lane = lax.broadcasted_iota(jnp.int32, (1, layout.columns), 1)
    own_slot = lane // layout.slot
    partner_slot = own_slot ^ params[2:3].astype(jnp.int32)
    return lax.rem(partner_slot - own_slot + layout.sections, layout.sections)


def store_slabs(fine, target):
    for q in range(MIRROR + 1):
        for point, slab in zip((q, FINE - 1 - q), fine_slabs(fine, q)):
            base = 0
            for part in slab:
                target[point, pl.ds(base, part.shape[0]), :] = part
                base += part.shape[0]


def gradients(tall, pieces, fine):
    for direction in range(3):
        for index in range(4):
            source = index ^ (2 if direction == 0 else 1 if direction == 2 else 0)
            fine[direction][index][...] = multiply(
                lift_matrix(tall, direction + 1, index), pieces[source]
            )


def start_kernel(layout, tables, scalars, *refs):
    sections, columns = layout.sections, layout.columns
    here = scalars[0]
    refs = list(refs)

    def take(count):
        taken, refs[:] = refs[:count], refs[count:]
        return taken

    chunks, tips = take(sections), take(sections // 2)
    (iterate, param_value, keep, gain_k, gain, gain_low, gain_high, gain_wall) = take(8)
    unpack_field(layout, here, 0, chunks, 0, tips, iterate)
    params = unpack_params(layout, here, chunks, tips)
    param_value[...] = params
    weights, stiff_line = tables[3], np.diagonal(tables[2])
    k, metal, _, has_low, has_high = [params[row : row + 1] for row in range(5)]
    distance = wall_distance(layout, params)
    coef_low = has_low * (0.5 * penalty) * (k + shifted(k, 1))
    coef_high = has_high * (0.5 * penalty) * (k + shifted(k, -1))
    partner_k, partner_metal = jnp.zeros_like(k), jnp.zeros_like(k)
    for step in range(1, sections):
        chosen = distance == step
        partner_k = jnp.where(chosen, shifted(k, -step * layout.slot), partner_k)
        partner_metal = jnp.where(chosen, shifted(metal, -step * layout.slot), partner_metal)
    coef_wall = jnp.where(metal != partner_metal, (0.5 * penalty) * (k + partner_k), 0.0)
    weight_b = column_weights(weights, columns)
    stiff_b = column_weights(stiff_line, columns)
    last = LINE_POINT_TOTAL - 1
    for a in range(LINE_POINT_TOTAL):
        for c in range(LINE_POINT_TOTAL):
            wa, wc = float(weights[a]), float(weights[c])
            mass = weight_b * (wa * wc / time_step)
            diag = mass + k * (
                weight_b * (float(stiff_line[a]) * wc + wa * float(stiff_line[c]))
                + stiff_b * (wa * wc)
            )
            face = None
            if a == 0:
                face_low = coef_low * (weight_b * wc)
                face = face_low
            if a == last:
                face_high = coef_high * (weight_b * wc)
                face = face_high
            if c == 0:
                face_wall = coef_wall * (weight_b * wa)
                face = face_wall if face is None else face + face_wall
            if face is not None:
                diag = diag + face
            factor = relaxation / diag
            span = pl.ds((a * 8 + c) * 8, 8)
            gain[span, :] = factor
            gain_k[span, :] = factor * k
            keep[span, :] = 1.0 - factor * (mass if face is None else mass + face)
            if a == 0:
                gain_low[pl.ds(c * 8, 8), :] = factor * face_low
            if a == last:
                gain_high[pl.ds(c * 8, 8), :] = factor * face_high
            if c == 0:
                gain_wall[pl.ds(a * 8, 8), :] = factor * face_wall


def relax(layout, factors, distance, current, pieces, results, tall, right_side, target):
    _, keep, gain_k, _, gain_low, gain_high, gain_wall = factors
    last = LINE_POINT_TOTAL - 1
    for index in range(4):
        stiff = tall.at[pl.ds(TALL[16 + index], 2 * CLASS_ROWS)]
        results[index] = multiply(stiff, pieces[index])
    from_low = gain_low[...] * shifted(current[pl.ds(last * 64, 64), :], 1)
    from_high = gain_high[...] * shifted(current[pl.ds(0, 64), :], -1)
    wall = jnp.concatenate([current[pl.ds(a * 64, 8), :] for a in range(8)], 0)
    far = jnp.zeros_like(wall)
    for step in range(1, layout.sections):
        far = jnp.where(distance == step, shifted(wall, -step * layout.slot), far)
    from_wall = gain_wall[...] * far
    for a in range(HALF):
        for plane, stiffness in zip((a, last - a), from_classes(results, a)):
            span = pl.ds(plane * 64, 64)
            value = keep[span, :] * current[span, :] - gain_k[span, :] * stiffness
            if right_side is not None:
                value = value + right_side[span, :]
            if plane == 0:
                value = value + from_low
            if plane == last:
                value = value + from_high
            at_wall = value[:8] + from_wall[plane * 8 : plane * 8 + 8]
            target[span, :] = jnp.concatenate([at_wall, value[8:]], 0)


def slope_kernel(layout, scalars, *refs):
    (iterate, *factors), tall, slopes, first = refs[:8], refs[8], refs[9:12], refs[12]
    results, refs = refs[13], refs[14:]
    fine, pieces = [refs[4 * d : 4 * d + 4] for d in range(3)], refs[12:16]
    to_classes(iterate, pieces)
    gradients(tall, pieces, fine)
    for direction in range(3):
        store_slabs(fine[direction], slopes[direction])
    distance = wall_distance(layout, factors[0][...])
    relax(layout, factors, distance, iterate, pieces, results, tall, None, first)


def point_slabs(source, q):
    slabs = []
    for point in (q, FINE - 1 - q)[: 1 if q == MIRROR else 2]:
        slabs.append(
            [
                source[point, pl.ds(0, PAIR_ROWS), :],
                source[point, pl.ds(PAIR_ROWS, PAIR_ROWS), :],
                source[point, pl.ds(2 * PAIR_ROWS, MID_ROWS), :],
            ]
        )
    return slabs


def add_products(total, slabs, others):
    terms = [[x * y for x, y in zip(s, t)] for s, t in zip(slabs, others)]
    if total is None:
        return terms
    return [[x + y for x, y in zip(s, t)] for s, t in zip(total, terms)]


def project(layout, products_of, wide, fine_pieces, results):
    pending = [[], [], [], []]
    done = [0, 0, 0, 0]
    for q in range(MIRROR + 1):
        products = products_of(q)
        halves = products
        if len(products) == 2:
            halves = [
                [x + y for x, y in zip(*products)],
                [x - y for x, y in zip(*products)],
            ]
        for parity_a, (plus, minus, middle) in enumerate(halves):
            pending[2 * parity_a] += [plus + minus, middle]
            pending[2 * parity_a + 1].append(plus - minus)
        for index, cls in enumerate(CLASSES):
            held = sum(part.shape[0] for part in pending[index])
            final = q >= FINE_A_COUNT[cls[0]] - 1
            if pending[index] and (held % 16 == 0 or final):
                if held % 16:
                    pending[index].append(jnp.zeros((8, layout.columns), jnp.float32))
                    held += 8
                store_split(
                    fine_pieces[index],
                    done[index],
                    class_fine_rows(cls),
                    jnp.concatenate(pending[index], 0),
                )
                done[index] += held
                pending[index] = []
    for index in range(4):
        back = wide.at[:, pl.ds(WIDE[index], HEIGHTS[index])]
        results[index] = multiply(back, fine_pieces[index])


def march_kernel(layout, tables, scalars, *refs):
    weights = tables[3]
    sections, columns = layout.sections, layout.columns
    refs = list(refs)

    def take(count):
        taken, refs[:] = refs[:count], refs[count:]
        return taken

    chunks, tips = [take(sections) for _ in PARTS], take(sections // 2)
    (initial, *factors), slopes = take(8), take(3)
    (first, tall, wide) = take(3)
    outs = take(sections)
    (iterate, results, gain_rhs) = take(3)
    lifted = take(3)
    fine, pieces, fine_pieces = [take(4) for _ in range(3)], take(4), take(4)

    for d in range(3):
        part = next(index for index, inside in enumerate(PARTS) if 1 + d in inside)
        base = PARTS[part].index(1 + d) * layout.chunk_rows
        planes = unpack_field(layout, scalars[0], 1 + d, chunks[part], base, tips, None)
        to_classes(planes, pieces)
        for index in range(4):
            fine[0][index][...] = multiply(lift_matrix(tall, 0, index), pieces[index])
        store_slabs(fine[0], lifted[d])
    gain, params = factors[3], factors[0][...]
    distance = wall_distance(layout, params)
    fluid = 1.0 - params[1:2]
    weight_b = column_weights(weights, columns)
    last = LINE_POINT_TOTAL - 1

    def first_products(q):
        total = None
        for slope, velocity in zip(slopes, lifted):
            total = add_products(total, point_slabs(slope, q), point_slabs(velocity, q))
        return total

    def later_products(q):
        total = None
        for slope, velocity in zip(fine, lifted):
            total = add_products(total, fine_slabs(slope, q), point_slabs(velocity, q))
        return total

    for step_index in range(STEPS):
        current = initial if step_index == 0 else iterate
        if step_index == 0:
            project(layout, first_products, wide, fine_pieces, results)
        else:
            to_classes(current, pieces)
            gradients(tall, pieces, fine)
            project(layout, later_products, wide, fine_pieces, results)
        for a in range(HALF):
            for plane, convected in zip((a, last - a), from_classes(results, a)):
                for c in range(LINE_POINT_TOTAL):
                    span = pl.ds((plane * 8 + c) * 8, 8)
                    mass = weight_b * float(weights[plane] * weights[c] / time_step)
                    right_side = gain[span, :] * (
                        mass * current[span, :] - fluid * convected[c * 8 : c * 8 + 8]
                    )
                    gain_rhs[span, :] = right_side
                    if step_index == 0:
                        iterate[span, :] = first[span, :] + right_side
        for sweep_index in range(1 if step_index == 0 else 0, SWEEPS):
            if sweep_index > 0:
                to_classes(iterate, pieces)
            relax(
                layout, factors, distance, iterate, pieces, results, tall, gain_rhs, iterate
            )

    rows = layout.main_rows
    lane = lane_iota(rows)
    for section in range(sections):
        value = jnp.zeros((rows, LANES), jnp.float32)
        for group in range(sections):
            for tile, _, shift, first, last_lane in layout.window_pieces(
                section * layout.slot + GHOST, group * layout.main, layout.main
            ):
                block = iterate[pl.ds(group * rows, rows), pl.ds(tile * LANES, LANES)]
                value = jnp.where(in_range(lane, first, last_lane), turned(block, shift), value)
        outs[section][...] = value


def gather_kernel(layout, scalars, *refs):
    chunks, (out, held, sent) = refs[: layout.sections], refs[layout.sections :]
    here = scalars[0]
    rows, main, elements = layout.main_rows, layout.main, layout.elements
    lane = lane_iota(rows)
    sections = layout.sections
    held_chunks = [
        pltpu.roll(chunks[shift][...], lax.rem((here ^ shift) * main, elements), axis=1)
        for shift in range(sections)
    ]
    copies = []
    for group in range(sections):
        wanted = (lane // main + (sections - group)) % sections ^ here
        value = held_chunks[0]
        for shift in range(1, sections):
            value = jnp.where(wanted == shift, held_chunks[shift], value)
        value = turned(value, -group * main)
        for index in range(rows // 8):
            a, c = divmod(group * (rows // 8) + index, LINE_POINT_TOTAL)
            held[pl.ds(a * 64 + c, 8, stride=8), :] = value[index * 8 : index * 8 + 8]
        planes = (group + 1) * rows // 64
        if planes > group * rows // 64:
            span = pl.ds((planes - max(1, rows // 64)) * 64, max(64, rows))
            copy = pltpu.make_async_copy(held.at[span], out.at[span], sent.at[group])
            copy.start()
            copies.append(copy)
    for copy in copies:
        copy.wait()


def shape_of(*dims, dtype=jnp.float32):
    return jax.ShapeDtypeStruct(dims, dtype)


def in_vmem(count):
    return [pl.BlockSpec(memory_space=pltpu.VMEM)] * count


def in_hbm(count):
    return [pl.BlockSpec(memory_space=pltpu.HBM)] * count


def kept_in_hbm(array):
    return pltpu.with_memory_space_constraint(array, pltpu.HBM)


FLOPS_BUSY = 1e8


SCALAR = pl.BlockSpec(memory_space=pltpu.SMEM)
PARAMS = pltpu.CompilerParams(vmem_limit_bytes=24 * 1024 * 1024)


def body(
    thermal_level_points,
    flow_speed_vector,
    thermal_diffusivity_cell,
    metal_cell_indicator,
    adjoining_patch,
):
    sections = lax.axis_size("sec")
    blocks = lax.axis_size("elem")
    elements = thermal_diffusivity_cell.shape[1]
    layout = Layout(elements, sections)
    scalars = jnp.stack([lax.axis_index("sec"), lax.axis_index("elem")]).astype(jnp.int32)
    f32, bf16 = jnp.float32, jnp.bfloat16
    dma = pltpu.SemaphoreType.DMA

    columns = layout.columns

    def call(kernel, name, out_shape, arrays, hbm=(), scratch=(), out_specs=None, busy=1.0):
        results = pl.pallas_call(
            kernel,
            out_shape=out_shape,
            in_specs=[SCALAR] + in_vmem(len(arrays)) + in_hbm(len(hbm)),
            out_specs=in_vmem(len(out_shape)) if out_specs is None else out_specs,
            scratch_shapes=list(scratch),
            compiler_params=PARAMS,
            cost_estimate=pl.CostEstimate(
                flops=int(busy * FLOPS_BUSY), bytes_accessed=0, transcendentals=0
            ),
            name=name,
        )(scalars, *arrays, *[kept_in_hbm(array) for array in hbm])
        return list(results)

    chunk_shapes = [
        shape_of(len(fields) * layout.chunk_rows + extra, elements)
        for fields, extra in (
            (PARTS[0], PARAM_ROWS + 2 * layout.tips_rows),
            (PARTS[0], PARAM_ROWS),
            *((fields, 0) for fields in PARTS[1:] for _ in range(2)),
        )
    ]
    packed = call(
        functools.partial(pack_kernel, layout, blocks),
        "pack",
        chunk_shapes,
        [],
        hbm=[
            thermal_level_points.reshape(POINTS, elements),
            flow_speed_vector.reshape(3, POINTS, elements),
            thermal_diffusivity_cell,
            metal_cell_indicator,
            adjoining_patch,
        ],
        scratch=[
            pltpu.VMEM((POINTS, elements), f32),
            pltpu.VMEM((3, POINTS, elements), f32),
            pltpu.VMEM((1, elements), f32),
            pltpu.VMEM((1, elements), jnp.int32),
            pltpu.VMEM((1, elements), jnp.int32),
            pltpu.VMEM((layout.units, layout.unit_rows, elements), f32),
            dma((7,)),
        ],
        busy=3.3,
    )

    def across(array, mask):
        return lax.ppermute(array, "sec", [(i, i ^ mask) for i in range(sections)])

    chunks = [
        {0: packed[2 * part], layout.half: across(packed[2 * part + 1], layout.half)}
        for part in range(len(PARTS))
    ]
    chunks[0][1] = across(packed[0], 1)
    early, late = call(
        functools.partial(join_kernel, layout),
        "join",
        [shape_of(2 * layout.tips_rows, elements)] * 2,
        [chunks[0][0], chunks[0][1]],
        busy=0.6,
    )
    tips = []
    for step in range(sections // 2):
        mirrored = sections // 2 - 1 - step
        up, down = 2 * step + 1, 2 * mirrored + 1
        pairs = [(up * blocks + i, i + 1) for i in range(blocks - 1)]
        pairs += [
            (down * blocks + i + 1, (sections - 1) * blocks + i) for i in range(blocks - 1)
        ]
        tips.append(
            lax.ppermute(early if step < sections // 4 else late, ("sec", "elem"), pairs)
        )
    def spread(chunk, after):
        chunk[layout.half], after = lax.optimization_barrier((chunk[layout.half], after))
        bit = layout.half // 2
        while bit:
            for mask in sorted(chunk):
                if mask | bit not in chunk:
                    chunk[mask | bit] = across(chunk[mask], bit)
            bit //= 2
        return [chunk[mask] for mask in range(sections)], after

    chunks[0], tips = spread(chunks[0], tips)

    lifts, backs, stiff = make_matrices()
    tall = jnp.asarray(np.concatenate(lifts + stiff, 0))
    wide = jnp.asarray(
        np.concatenate(
            [
                np.pad(back, ((0, 0), (0, round_up(back.shape[1], LANES) - back.shape[1])))
                for back in backs
            ],
            1,
        )
    )
    tables = make_tables()
    fine_rows = [class_fine_rows(cls) for cls in CLASSES]
    points = shape_of(POINTS, columns)
    fine_field = shape_of(FINE, SLAB_ROWS, columns)
    face = shape_of(64, columns)
    fine_scratch = [pltpu.VMEM((rows, columns), f32) for rows in fine_rows]
    piece_scratch = [pltpu.VMEM((2 * CLASS_ROWS, columns), bf16) for _ in CLASSES]
    started = call(
        functools.partial(start_kernel, layout, tables),
        "start",
        [points, shape_of(PARAM_ROWS, columns)]
        + [points] * 3
        + [face] * 3,
        chunks[0] + tips,
        busy=15.0,
    )
    factors = started
    chunks[1][0], factors[1] = lax.optimization_barrier((chunks[1][0], factors[1]))
    *slopes, first = call(
        functools.partial(slope_kernel, layout),
        "slope",
        [fine_field] * 3 + [points],
        factors + [tall],
        scratch=[pltpu.VMEM((4, CLASS_ROWS, columns), f32)] + fine_scratch * 3 + piece_scratch,
        busy=15.0,
    )
    chunks[1], slopes[0] = spread(chunks[1], slopes[0])
    results = call(
        functools.partial(march_kernel, layout, tables),
        "march",
        [shape_of(layout.main_rows, elements)] * sections,
        chunks[0] + chunks[1] + tips + factors + slopes + [first, tall, wide],
        scratch=[
            pltpu.VMEM((POINTS, columns), f32),
            pltpu.VMEM((4, CLASS_ROWS, columns), f32),
            pltpu.VMEM((POINTS, columns), f32),
            *[pltpu.VMEM((FINE, SLAB_ROWS, columns), f32) for _ in range(3)],
            *(fine_scratch * 3),
            *piece_scratch,
            *[pltpu.VMEM((2 * rows, columns), bf16) for rows in fine_rows],
        ],
        busy=8.9,
    )
    results = [results[0]] + [across(results[mask], mask) for mask in range(1, sections)]
    (result,) = call(
        functools.partial(gather_kernel, layout),
        "unpack",
        [shape_of(POINTS, elements)],
        list(results),
        scratch=[pltpu.VMEM((POINTS, elements), f32), dma((sections,))],
        out_specs=in_hbm(1),
        busy=1.5,
    )
    return result.reshape(thermal_level_points.shape)


def solution(mesh):
    return jax.shard_map(
        body,
        mesh=mesh,
        in_specs=(
            P("sec", None, None, None, "elem"),
            P(None, "sec", None, None, None, "elem"),
            P("sec", "elem"),
            P("sec", "elem"),
            P("sec", "elem"),
        ),
        out_specs=P("sec", None, None, None, "elem"),
        check_vma=False,
    )
```
